512 devices in a mesh: seq: 64 (over z, y), kvh: 8 (over x, core).
Axes of the slice: x: 4, y: 8, z: 8, core: 2. Of those that a mesh axis runs over, the one named last changes fastest.
Arguments:
- queries: bfloat16 [128, 8192], P(None, 'kvh'), may hold values from -256 to 256
- new_keys: bfloat16 [128, 1024], P(None, 'kvh'), may hold values from -40 to 40
- new_values: bfloat16 [128, 1024], P(None, 'kvh'), may hold values from -6 to 6
- prefix_keys: bfloat16 [131072, 1024], P('seq', 'kvh'), may hold values from -8 to 8
- prefix_values: bfloat16 [131072, 1024], P('seq', 'kvh'), may hold values from -6 to 6
- suffix_keys: bfloat16 [128, 1024, 1024], P(None, 'seq', 'kvh'), may hold values from -16 to 16
- suffix_values: bfloat16 [128, 1024, 1024], P(None, 'seq', 'kvh'), may hold values from -6 to 6
- prefix_offsets: int32 [128], replicated, may hold values from 2 to 131072, as said below
- suffix_lengths: int32 [128], replicated, may hold values from 0 to 1024, as said below
- out_weight: bfloat16 [8192, 8192], P('kvh', 'seq'), may hold values from -0.0625 to 0.0625
- residual: bfloat16 [128, 8192], P(None, 'seq'), may hold values from -70 to 70
- norm_gain: float32 [8192], P('seq'), may hold values from 0.1 to 1.9
- w_gate: bfloat16 [8192, 28672], P('seq', 'kvh'), may hold values from -0.0625 to 0.0625
- w_up: bfloat16 [8192, 28672], P('seq', 'kvh'), may hold values from -0.0625 to 0.0625
- w_down: bfloat16 [28672, 8192], P('kvh', 'seq'), may hold values from -0.03125 to 0.03125
Outputs:
- attention: bfloat16 [128, 8192], P(None, 'kvh')
- mixed: bfloat16 [128, 8192], P(None, 'seq')
The draws below stay inside these ranges and needn't reach their ends.
Inputs may be any that keep to these rules, and one draw needn't show every extreme that they name: Branch b sees the prefix positions below prefix_offsets[b]; some branch sees all 131072. Branch b's suffix positions below suffix_lengths[b] are live; some branch has all 1024.
All inputs are finite; a program needn't handle non-finite values.
Results may differ from the reference program's by a relative error of at most 0.007.
Values may be sent and summed in bfloat16 or wider, within the bound.
No kernel may reach another device: no remote copies, remote signals or barrier semaphores. Data moves between devices by JAX's collectives and lax.ppermute only.
A program may use at most 192 MiB of HBM per device.

```python
import math
import jax
import jax.numpy as jnp
from jax import lax

D = 8192
H = 64
KVH = 8
HD = 128
FF = 28672
B = 128
CTX_DEV = 2048
SUF_DEV = 16
PREFIX = 131072
SUF = 1024
N_SEQ = 64


def query_noise(key):
    return jnp.clip(jax.random.normal(jax.random.fold_in(key, 101), (B, H * HD), jnp.float32), -6.0, 6.0)


def anchor_keys(key):
    return jnp.clip(jax.random.normal(jax.random.fold_in(key, 102), (KVH, HD), jnp.float32), -6.0, 6.0)


def shared_direction(key):
    per_group = H // KVH
    query_base = query_noise(key)
    return jnp.mean(query_base.reshape(B, KVH, per_group, HD), axis=2).reshape(B, KVH * HD)


def draw_queries(key, part):
    query_base = query_noise(key)
    anchors = anchor_keys(key)
    key = jax.random.fold_in(key, 1)
    scale_key, level_key = jax.random.split(key, 2)
    lowest = 2.0
    levels = jnp.array([0.0, 0.0, 24.0, 32.0], jnp.float32)
    row_scale = jnp.exp(jax.random.uniform(scale_key, (B, 1, 1, 1), jnp.float32, math.log(lowest), math.log(40.0)))
    strength = levels[jax.random.randint(level_key, (B,), 0, 4)]
    entries = row_scale * query_base.reshape(B, KVH, H // KVH, HD) + strength[:, None, None, None] * anchors[None, :, None, :]
    entries = jnp.clip(entries.reshape(B, H * HD), -256.0, 256.0)
    return entries.astype(jnp.bfloat16)


def draw_new_keys(key, part):
    shared = shared_direction(key)
    key = jax.random.fold_in(key, 2)
    own_part = jnp.clip(jax.random.normal(key, (B, KVH * HD), jnp.float32), -6.0, 6.0)
    per_group = H // KVH
    coupling = per_group * math.sqrt(2.0 * math.log(PREFIX)) / math.sqrt(HD)
    return (own_part + coupling * shared).astype(jnp.bfloat16)


def draw_suffix_keys(key, part):
    shared = shared_direction(key)
    key = jax.random.fold_in(key, 7)
    own_part = jnp.clip(jax.random.normal(key, (B, SUF, KVH * HD), jnp.float32), -6.0, 6.0)
    per_group = H // KVH
    coupling = 0.3 * per_group * math.sqrt(2.0 * math.log(PREFIX)) / math.sqrt(HD)
    entries = jnp.clip(own_part + coupling * shared[:, None, :], -16.0, 16.0)
    return entries.astype(jnp.bfloat16)


def draw_prefix_keys(key, part):
    anchors = anchor_keys(key).reshape(1, KVH * HD)
    key = jax.random.fold_in(key, 3)
    entries = jnp.clip(jax.random.normal(key, (PREFIX, KVH * HD), jnp.float32), -6.0, 6.0)
    entries = entries.at[0:2].set(jnp.concatenate([anchors, 0.991 * anchors], axis=0))
    return entries.astype(jnp.bfloat16)


def draw_prefix_offsets(key, part):
    key = jax.random.fold_in(key, 4)
    first_key, second_key = jax.random.split(key, 2)
    offsets = jax.random.randint(first_key, (B,), 2, PREFIX + 1)
    chosen = jax.random.randint(second_key, (), 0, B)
    return offsets.at[chosen].set(PREFIX).astype(jnp.int32)


def draw_suffix_lengths(key, part):
    key = jax.random.fold_in(key, 5)
    first_key, second_key = jax.random.split(key, 2)
    counts = jax.random.randint(first_key, (B,), 0, SUF + 1)
    chosen = jax.random.randint(second_key, (), 0, B)
    return counts.at[chosen].set(SUF).astype(jnp.int32)


def draw_residual(key, part):
    key = jax.random.fold_in(key, 6)
    row_key, column_key, entry_key = jax.random.split(key, 3)
    row_scale = jnp.exp(jax.random.uniform(row_key, (B, 1), jnp.float32, math.log(0.3), math.log(3.0)))
    rising = 0.5 + jnp.arange(D, dtype=jnp.float32)[None, :] / D
    column_scale = jnp.exp(jax.random.uniform(column_key, (1, D), jnp.float32, math.log(0.3), math.log(3.0))) * rising
    entries = jax.random.normal(entry_key, (B, D), jnp.float32)
    entries = jnp.clip(entries, -5.0, 5.0)
    return (entries * row_scale * column_scale).astype(jnp.bfloat16)


def level_of(own_key, dims, cuts, smallest, high):
    def one(dim, blocks):
        steps = jax.random.uniform(jax.random.fold_in(jax.random.fold_in(own_key, 6), dim), (blocks,), jnp.float32, smallest / len(cuts), high / len(cuts))
        return jnp.repeat(jnp.exp(steps), dims[dim] // blocks).reshape((-1,) + (1,) * (len(dims) - dim - 1))

    level = one(*cuts[0])
    for cut in cuts[1:]:
        level = level * one(*cut)
    return level


def gaussian(rng, shape, spread, bound, cuts=(), kind=jnp.bfloat16):
    result = jax.random.normal(rng, shape, jnp.float32) * spread
    if len(cuts) > 0:
        result = level_of(rng, shape, cuts, -0.22, 0.18) * result
    return jnp.clip(result, min=-bound, max=bound).astype(kind)


def setup_inputs(seed: int = 0) -> dict:
    arg_keys = jax.random.split(jax.random.key(seed), 16)
    queries = draw_queries(jax.random.fold_in(arg_keys[15], 71), 0)
    new_keys = draw_new_keys(jax.random.fold_in(arg_keys[15], 71), 0)
    new_values = gaussian(arg_keys[2], (B, KVH * HD), 1.0, 6.0, ((1, 8),))
    prefix_keys = draw_prefix_keys(jax.random.fold_in(arg_keys[15], 71), 0)
    prefix_values = gaussian(arg_keys[4], (PREFIX, KVH * HD), 1.0, 6.0, ((0, 64), (1, 8)))
    suffix_keys = draw_suffix_keys(jax.random.fold_in(arg_keys[15], 71), 0)
    suffix_values = gaussian(arg_keys[6], (B, SUF, KVH * HD), 1.0, 6.0, ((1, 64), (2, 8)))
    prefix_offsets = draw_prefix_offsets(jax.random.fold_in(arg_keys[15], 71), 0)
    suffix_lengths = draw_suffix_lengths(jax.random.fold_in(arg_keys[15], 71), 0)
    out_weight = gaussian(arg_keys[9], (H * HD, D), (H * HD) ** -0.5, 0.0625, ((0, 8), (1, 64)))
    residual = draw_residual(jax.random.fold_in(arg_keys[15], 71), 0)
    norm_gain = jnp.clip(1.0 + 0.18 * jax.random.normal(arg_keys[11], (D,), jnp.float32), 0.1, 1.9)
    w_gate = gaussian(arg_keys[12], (D, FF), D ** -0.5, 0.0625, ((0, 64), (1, 8)))
    w_up = gaussian(arg_keys[13], (D, FF), D ** -0.5, 0.0625, ((0, 64), (1, 8)))
    w_down = gaussian(arg_keys[14], (FF, D), FF ** -0.5, 0.03125, ((0, 8), (1, 64)))
    return dict(queries=queries, new_keys=new_keys, new_values=new_values, prefix_keys=prefix_keys, prefix_values=prefix_values, suffix_keys=suffix_keys, suffix_values=suffix_values, prefix_offsets=prefix_offsets, suffix_lengths=suffix_lengths, out_weight=out_weight, residual=residual, norm_gain=norm_gain, w_gate=w_gate, w_up=w_up, w_down=w_down)


NEG_FILL = -1e+30
EPSILON = 1e-05

def block_partial(query_heads, keys_block, values_block, keys_tail, values_tail, live_block, live_tail):
    score_scale = 1.0 / math.sqrt(HD)
    prefix_scores = jnp.einsum('bghd,pgd->bghp', query_heads, keys_block.astype(jnp.float32)) * score_scale
    tail_scores = jnp.einsum('bghd,btgd->bght', query_heads, keys_tail.astype(jnp.float32)) * score_scale
    prefix_live = live_block[:, None, None, :]
    tail_live = live_tail[:, None, None, :]
    prefix_scores = jnp.where(prefix_live, prefix_scores, NEG_FILL)
    tail_scores = jnp.where(tail_live, tail_scores, NEG_FILL)
    block_peak = jnp.maximum(lax.optimization_barrier(jnp.max(prefix_scores, axis=-1)), lax.optimization_barrier(jnp.max(tail_scores, axis=-1)))
    prefix_weights = jnp.where(prefix_live, jnp.exp(prefix_scores - block_peak[..., None]), 0.0).astype(jnp.bfloat16)
    tail_weights = jnp.where(tail_live, jnp.exp(tail_scores - block_peak[..., None]), 0.0).astype(jnp.bfloat16)
    prefix_wide = prefix_weights.astype(jnp.float32)
    tail_wide = tail_weights.astype(jnp.float32)
    block_total = lax.optimization_barrier(jnp.sum(prefix_wide, axis=-1)) + lax.optimization_barrier(jnp.sum(tail_wide, axis=-1))
    block_output = jnp.einsum('bghp,pgd->bghd', prefix_wide, values_block.astype(jnp.float32))
    block_output = block_output + jnp.einsum('bght,btgd->bghd', tail_wide, values_tail.astype(jnp.float32))
    return (block_peak, block_total, block_output)

def reference(queries, new_keys, new_values, prefix_keys, prefix_values, suffix_keys, suffix_values, prefix_offsets, suffix_lengths, out_weight, residual, norm_gain, w_gate, w_up, w_down):
    branches = queries.shape[0]
    per_group = H // KVH
    score_scale = 1.0 / math.sqrt(HD)
    query_heads = queries.astype(jnp.float32).reshape(branches, KVH, per_group, HD)
    key_blocks = prefix_keys.reshape(N_SEQ, CTX_DEV, KVH, HD)
    value_blocks = prefix_values.reshape(N_SEQ, CTX_DEV, KVH, HD)
    tail_keys = suffix_keys.reshape(branches, N_SEQ, SUF_DEV, KVH, HD).transpose(1, 0, 2, 3, 4)
    tail_values = suffix_values.reshape(branches, N_SEQ, SUF_DEV, KVH, HD).transpose(1, 0, 2, 3, 4)
    block_ids = jnp.arange(N_SEQ, dtype=jnp.int32)

    def one_block(items):
        keys_block, values_block, keys_tail, values_tail, block_index = items
        prefix_pos = block_index * CTX_DEV + jnp.arange(CTX_DEV, dtype=jnp.int32)
        tail_pos = block_index * SUF_DEV + jnp.arange(SUF_DEV, dtype=jnp.int32)
        live_block = prefix_pos[None, :] < prefix_offsets[:, None]
        live_tail = tail_pos[None, :] < suffix_lengths[:, None]
        return block_partial(query_heads, keys_block, values_block, keys_tail, values_tail, live_block, live_tail)
    block_peaks, block_totals, block_outputs = lax.map(one_block, (key_blocks, value_blocks, tail_keys, tail_values, block_ids))
    new_scores = jnp.einsum('bghd,bgd->bgh', query_heads, new_keys.astype(jnp.float32).reshape(branches, KVH, HD)) * score_scale
    row_peak = jnp.maximum(lax.optimization_barrier(jnp.max(block_peaks, axis=0)), new_scores)
    factors = jnp.exp(block_peaks - row_peak[None])
    fresh_factor = jnp.exp(new_scores - row_peak)
    fresh_values = new_values.astype(jnp.float32).reshape(branches, KVH, 1, HD)
    numerator = lax.optimization_barrier(jnp.sum(factors[..., None] * block_outputs, axis=0)) + fresh_factor[..., None] * fresh_values
    denominator = lax.optimization_barrier(jnp.sum(factors * block_totals, axis=0)) + fresh_factor
    attention = (numerator / denominator[..., None]).astype(jnp.bfloat16).reshape(branches, H * HD)
    projected = jnp.dot(attention, out_weight, preferred_element_type=jnp.float32)
    hidden_state = (residual.astype(jnp.float32) + projected).astype(jnp.bfloat16)
    hidden_wide = hidden_state.astype(jnp.float32)
    mean_square = lax.optimization_barrier(jnp.sum(hidden_wide * hidden_wide, axis=1)) / D
    normed = (hidden_wide * lax.rsqrt(mean_square + EPSILON)[:, None] * norm_gain).astype(jnp.bfloat16)
    gate_sum = jnp.dot(normed, w_gate, preferred_element_type=jnp.float32)
    up_sum = jnp.dot(normed, w_up, preferred_element_type=jnp.float32)
    activation = (jax.nn.silu(gate_sum) * up_sum).astype(jnp.bfloat16)
    ffn_sum = jnp.dot(activation, w_down, preferred_element_type=jnp.float32)
    mixed = (hidden_wide + ffn_sum).astype(jnp.bfloat16)
    return (attention, mixed)
```

```python
import functools
import math

import jax
import jax.numpy as jnp
from jax import lax
from jax.experimental import pallas as pl
from jax.experimental.pallas import tpu as pltpu
from jax.sharding import PartitionSpec as P

HD = 128
NEG_FILL = -1e30
EPSILON = 1e-05
SCALE_LOG2 = math.log2(math.e) / math.sqrt(HD)
ONES = 16
STATS = 8


def dot_nt(a, b):
    return lax.dot_general(a, b, (((1,), (1,)), ((), ())), preferred_element_type=jnp.float32)


def parts_of(x, count):
    parts = []
    for _ in range(count):
        part = x.astype(jnp.bfloat16).astype(jnp.float32)
        parts.append(part)
        x = x - part
    return parts


def with_ones(values):
    return jnp.concatenate(
        [values.T, jnp.ones((ONES, values.shape[0]), values.dtype)], axis=0
    )


def attend(bands, band, heads, off_ref, len_ref, q_ref, k_ref, v_ref, sk_ref, sv_ref, out_ref,
           stat_ref, vt_ref):
    context = k_ref.shape[0]
    tail = sk_ref.shape[1]
    cols = heads * band
    seq = lax.axis_index("seq")
    vt_ref[...] = with_ones(v_ref[...])

    def queries_of(g):
        block = q_ref[pl.ds(pl.multiple_of(g * band, band), band), :]
        return jnp.concatenate([block[:, h * HD : (h + 1) * HD] for h in range(heads)], axis=0)

    def pair(p, carry):
        bases = (2 * p, 2 * p + 1)
        qs = [queries_of(g) for g in bases]
        both = jnp.concatenate(qs, axis=0)
        offset = jnp.concatenate([off_ref[pl.ds(g, 1), :] for g in bases], axis=1)
        scores = dot_nt(k_ref[...], both)
        pos = lax.broadcasted_iota(jnp.int32, scores.shape, 0)
        scores = jnp.where(pos < offset - seq * context, scores, NEG_FILL)
        peak = jnp.max(scores, axis=0, keepdims=True)
        tails = []
        for i, g in enumerate(bases):
            at = pl.multiple_of(g * band, band)
            keys = sk_ref[pl.ds(at, band)].reshape(band * tail, HD)
            tail_scores = dot_nt(keys, qs[i])
            row = lax.broadcasted_iota(jnp.int32, tail_scores.shape, 0)
            col = lax.broadcasted_iota(jnp.int32, tail_scores.shape, 1)
            length = len_ref[pl.ds(g, 1), :] - seq * tail
            live = (row // tail == col % band) & (row % tail < length)
            tails.append(jnp.where(live, tail_scores, NEG_FILL))
        tail_peak = jnp.concatenate([jnp.max(t, axis=0, keepdims=True) for t in tails], axis=1)
        peak = jnp.maximum(peak, tail_peak)
        weights = jnp.exp2((scores - peak) * SCALE_LOG2).astype(jnp.bfloat16)
        sums = jnp.dot(vt_ref[...], weights, preferred_element_type=jnp.float32)
        for i, g in enumerate(bases):
            at = pl.multiple_of(g * band, band)
            own = slice(i * cols, (i + 1) * cols)
            own_peak = peak[:, own]
            tail_weights = jnp.exp2((tails[i] - own_peak) * SCALE_LOG2).astype(jnp.bfloat16)
            values = with_ones(sv_ref[pl.ds(at, band)].reshape(band * tail, HD))
            full = sums[:, own] + jnp.dot(values, tail_weights, preferred_element_type=jnp.float32)
            some = own_peak > 0.5 * NEG_FILL
            total = jnp.where(some, full[HD : HD + 1], 0.0)
            output = jnp.where(some, full[:HD], 0.0).T.astype(jnp.bfloat16)
            out_ref[pl.ds(pl.multiple_of(g * heads, heads), heads)] = output.reshape(heads, band, HD)
            rows = parts_of(own_peak, 3) + parts_of(total, 2)
            rows += [jnp.zeros_like(total)] * (STATS - len(rows))
            stat_ref[g] = jnp.concatenate(rows, axis=0)
        return carry

    lax.fori_loop(0, bands // 2, pair, 0)


def kvh_sum(x, n):
    sent = x.astype(jnp.bfloat16)
    total = sent.astype(jnp.float32)
    for step in range(1, n):
        got = lax.ppermute(sent, "kvh", [(i, (i + step) % n) for i in range(n)])
        total = total + got.astype(jnp.float32)
    return total


def on_device(n_seq, n_kvh, queries, new_keys, new_values, prefix_keys, prefix_values, suffix_keys,
              suffix_values, prefix_offsets, suffix_lengths, out_weight, residual, norm_gain,
              w_gate, w_up, w_down):
    branches = queries.shape[0]
    heads = queries.shape[1] // HD
    bands = n_seq // heads
    band = branches // bands
    hidden_units = w_gate.shape[1]
    width = n_seq * residual.shape[1]
    seq = lax.axis_index("seq")
    own_band, own_head = seq // heads, seq % heads

    by_column = lambda a: jnp.tile(a.reshape(bands, band), (1, heads))
    output, stats = pl.pallas_call(
        functools.partial(attend, bands, band, heads),
        out_shape=(
            jax.ShapeDtypeStruct((n_seq, band, HD), jnp.bfloat16),
            jax.ShapeDtypeStruct((bands, STATS, heads * band), jnp.float32),
        ),
        scratch_shapes=[pltpu.VMEM((HD + ONES, prefix_keys.shape[0]), jnp.bfloat16)],
        compiler_params=pltpu.CompilerParams(vmem_limit_bytes=40 * 2**20),
        name="attend",
    )(by_column(prefix_offsets), by_column(suffix_lengths), queries, prefix_keys, prefix_values,
      suffix_keys, suffix_values)
    stats = jnp.broadcast_to(stats.astype(jnp.bfloat16)[:, None], (bands, heads, STATS, heads * band))
    message = jnp.concatenate([output, stats.reshape(n_seq, STATS, heads * band)], axis=1)
    got = lax.all_to_all(message, "seq", 0, 0, tiled=True).astype(jnp.float32)

    own_stats = lax.dynamic_slice_in_dim(got[:, band:], own_head * band, band, axis=2)
    peaks = own_stats[:, 0] + own_stats[:, 1] + own_stats[:, 2]
    totals = own_stats[:, 3] + own_stats[:, 4]
    own_block = lambda a, col: lax.dynamic_slice(
        a, (own_band * band, col), (band, HD)
    ).astype(jnp.float32)
    own_queries = own_block(queries, own_head * HD)
    fresh = jnp.sum(own_queries * own_block(new_keys, 0), axis=1)
    row_peak = jnp.maximum(jnp.max(peaks, axis=0), fresh)
    factors = jnp.exp2((peaks - row_peak) * SCALE_LOG2)
    fresh_factor = jnp.exp2((fresh - row_peak) * SCALE_LOG2)
    numerator = jnp.sum(factors[:, :, None] * got[:, :band], axis=0)
    numerator += fresh_factor[:, None] * own_block(new_values, 0)
    denominator = jnp.sum(factors * totals, axis=0) + fresh_factor
    own_attention = (numerator / denominator[:, None]).astype(jnp.bfloat16)

    gathered = lax.all_gather(own_attention, "seq")
    attention = (
        gathered.reshape(bands, heads, band, HD).transpose(0, 2, 1, 3).reshape(branches, heads * HD)
    )

    projected = kvh_sum(jnp.dot(attention, out_weight, preferred_element_type=jnp.float32), n_kvh)
    hidden = (residual.astype(jnp.float32) + projected).astype(jnp.bfloat16)
    hidden_wide = hidden.astype(jnp.float32)
    squares = jnp.sum(hidden_wide * hidden_wide, axis=1)
    scaled = (hidden_wide * norm_gain).astype(jnp.bfloat16)
    by_unit = lambda w: lax.dot_general(
        w, scaled, (((0,), (1,)), ((), ())), preferred_element_type=jnp.float32
    ).astype(jnp.bfloat16).reshape(n_seq, hidden_units // n_seq, branches)
    coarse = lax.reduce_precision(squares, 8, 7)
    square_rows = jnp.stack([coarse, squares - coarse] + [jnp.zeros_like(squares)] * 6, axis=0)
    square_rows = jnp.broadcast_to(square_rows.astype(jnp.bfloat16), (n_seq, 8, branches))
    message = jnp.concatenate([by_unit(w_gate), by_unit(w_up), square_rows], axis=1)
    got = lax.all_to_all(message, "seq", 0, 0, tiled=True)
    sums = jnp.sum(got.astype(jnp.float32), axis=0)
    units = hidden_units // n_seq
    inverse = lax.rsqrt((sums[2 * units] + sums[2 * units + 1]) / width + EPSILON)
    activation = (jax.nn.silu(sums[:units] * inverse) * (sums[units : 2 * units] * inverse)).astype(
        jnp.bfloat16
    )
    copies = jnp.broadcast_to(activation, (n_seq, units, branches))
    activations = lax.all_to_all(copies, "seq", 0, 0, tiled=True).reshape(hidden_units, branches)
    ffn_part = lax.dot_general(
        activations, w_down, (((0,), (0,)), ((), ())), preferred_element_type=jnp.float32
    )
    mixed = (hidden_wide + kvh_sum(ffn_part, n_kvh)).astype(jnp.bfloat16)
    return (attention, mixed)


def solution(mesh):
    return jax.shard_map(
        functools.partial(on_device, mesh.shape["seq"], mesh.shape["kvh"]),
        mesh=mesh,
        in_specs=(
            P(None, "kvh"),
            P(None, "kvh"),
            P(None, "kvh"),
            P("seq", "kvh"),
            P("seq", "kvh"),
            P(None, "seq", "kvh"),
            P(None, "seq", "kvh"),
            P(),
            P(),
            P("kvh", "seq"),
            P(None, "seq"),
            P("seq"),
            P("seq", "kvh"),
            P("seq", "kvh"),
            P("kvh", "seq"),
        ),
        out_specs=(P(None, "kvh"), P(None, "seq")),
        check_vma=False,
    )
```

```python
import functools
import math

import jax
import jax.numpy as jnp
from jax import lax
from jax.experimental import pallas as pl
from jax.experimental.pallas import tpu as pltpu
from jax.sharding import PartitionSpec as P

HD = 128
D = 8192
SIDE = 8
Z_GROUPS = [[z * SIDE + y for z in range(SIDE)] for y in range(SIDE)]
Y_GROUPS = [[z * SIDE + y for y in range(SIDE)] for z in range(SIDE)]
NEG_FILL = -1e30
EPSILON = 1e-05
SCALE_LOG2 = math.log2(math.e) / math.sqrt(HD)
EXTRA = 16
PIECES = 4
MIB = 2**20


def dot_nt(a, b):
    return lax.dot_general(a, b, (((1,), (1,)), ((), ())), preferred_element_type=jnp.float32)


def parts_of(x, count):
    parts = []
    for _ in range(count):
        part = x.astype(jnp.bfloat16).astype(jnp.float32)
        parts.append(part)
        x = x - part
    return parts


def padded(rows, count):
    return jnp.concatenate(rows + [jnp.zeros_like(rows[0])] * (count - len(rows)), axis=0)


def with_ones(values):
    return jnp.concatenate([values.T, jnp.ones((EXTRA, values.shape[0]), values.dtype)], axis=0)


def bring(sources, targets, sems):
    waits = []
    for i, (source, target) in enumerate(zip(sources, targets)):
        size = source.shape[0] // PIECES
        copies = []
        for j in range(PIECES):
            part = pl.ds(j * size, size)
            copy = pltpu.make_async_copy(source.at[part], target.at[part], sems.at[i, j])
            copy.start()
            copies.append(copy)
        waits.append(lambda copies=copies: [copy.wait() for copy in copies])
    return waits


def head_rows(block, heads):
    return jnp.concatenate([block[:, h * HD : (h + 1) * HD] for h in range(heads)], axis=0)


def attend(bands, band, heads, off_ref, len_ref, q_ref, k_hbm, v_hbm, sk_hbm, sv_hbm, out_ref,
           k_ref, v_ref, sk_ref, sv_ref, vt_ref, sems):
    context = k_ref.shape[0]
    tail = sk_ref.shape[1]
    cols = heads * band
    seq = lax.axis_index("seq")
    waits = bring((k_hbm, v_hbm, sk_hbm, sv_hbm), (k_ref, v_ref, sk_ref, sv_ref), sems)
    waits[1]()
    vt_ref[...] = with_ones(v_ref[...])
    for i in (0, 2, 3):
        waits[i]()

    def queries_of(g):
        return head_rows(q_ref[pl.ds(pl.multiple_of(g * band, band), band), :], heads)

    def pair(p, carry):
        bases = (2 * p, 2 * p + 1)
        qs = [queries_of(g) for g in bases]
        both = jnp.concatenate(qs, axis=0)
        offset = jnp.concatenate([off_ref[pl.ds(g, 1), :] for g in bases], axis=1)
        scores = dot_nt(k_ref[...], both)
        pos = lax.broadcasted_iota(jnp.int32, scores.shape, 0)
        scores = jnp.where(pos < offset - seq * context, scores, NEG_FILL)
        peak = jnp.max(scores, axis=0, keepdims=True)
        tails = []
        for i, g in enumerate(bases):
            at = pl.multiple_of(g * band, band)
            keys = sk_ref[pl.ds(at, band)].reshape(band * tail, HD)
            tail_scores = dot_nt(keys, qs[i])
            row = lax.broadcasted_iota(jnp.int32, tail_scores.shape, 0)
            col = lax.broadcasted_iota(jnp.int32, tail_scores.shape, 1)
            length = len_ref[pl.ds(g, 1), :] - seq * tail
            live = (row // tail == col % band) & (row % tail < length)
            tails.append(jnp.where(live, tail_scores, NEG_FILL))
        tail_peak = jnp.concatenate([jnp.max(t, axis=0, keepdims=True) for t in tails], axis=1)
        peak = jnp.maximum(peak, tail_peak)
        weights = jnp.exp2((scores - peak) * SCALE_LOG2).astype(jnp.bfloat16)
        sums = jnp.dot(vt_ref[...], weights, preferred_element_type=jnp.float32)
        for i, g in enumerate(bases):
            at = pl.multiple_of(g * band, band)
            own = slice(i * cols, (i + 1) * cols)
            own_peak = peak[:, own]
            tail_weights = jnp.exp2((tails[i] - own_peak) * SCALE_LOG2).astype(jnp.bfloat16)
            values = with_ones(sv_ref[pl.ds(at, band)].reshape(band * tail, HD))
            full = sums[:, own] + jnp.dot(values, tail_weights, preferred_element_type=jnp.float32)
            some = own_peak > 0.5 * NEG_FILL
            total = jnp.where(some, full[HD : HD + 1], 0.0)
            output = jnp.where(some, full[:HD], 0.0).T
            stats = padded(parts_of(own_peak, 3) + parts_of(total, 2), EXTRA)
            out_ref[g] = jnp.concatenate([output, stats], axis=0).astype(jnp.bfloat16)
        return carry

    lax.fori_loop(0, bands // 2, pair, 0)


def merged(got_ref):
    count, rows = got_ref.shape[0], got_ref.shape[1] - EXTRA
    stats = [got_ref[s, rows:].astype(jnp.float32) for s in range(count)]
    peaks = [st[0:1] + st[1:2] + st[2:3] for st in stats]
    totals = [st[3:4] + st[4:5] for st in stats]
    peak = functools.reduce(jnp.maximum, peaks)
    factors = [jnp.exp2((p - peak) * SCALE_LOG2) for p in peaks]
    total = sum(f * t for f, t in zip(factors, totals))
    columns = padded(factors + [peak, total], rows).T
    output = sum(
        columns[:, s : s + 1] * got_ref[s, :rows].astype(jnp.float32) for s in range(count)
    )
    return output, peak, total, columns[:, count : count + 1], columns[:, count + 1 : count + 2]


def merge(got_ref, out_ref):
    output, peak, total, _, _ = merged(got_ref)
    stats = padded(parts_of(peak, 3) + parts_of(total, 2), EXTRA)
    message = jnp.concatenate([output, stats], axis=0).astype(jnp.bfloat16)
    for i in range(out_ref.shape[0]):
        out_ref[i] = message


def finish(heads, band, got_ref, q_ref, nk_ref, nv_ref, out_ref):
    output, _, _, peak, total = merged(got_ref)
    own = pl.ds(pl.multiple_of(lax.axis_index("seq") // SIDE * band, band), band)
    tiled = lambda ref: jnp.concatenate([ref[own, :].astype(jnp.float32)] * heads, axis=0)
    query = head_rows(q_ref[own, :], heads).astype(jnp.float32)
    fresh = jnp.sum(query * tiled(nk_ref), axis=1, keepdims=True)
    row_peak = jnp.maximum(peak, fresh)
    factor = jnp.exp2((peak - row_peak) * SCALE_LOG2)
    fresh_factor = jnp.exp2((fresh - row_peak) * SCALE_LOG2)
    numerator = factor * output + fresh_factor * tiled(nv_ref)
    attention = (numerator / (factor * total + fresh_factor)).astype(jnp.bfloat16)
    for i in range(out_ref.shape[0]):
        out_ref[i] = attention


def arrange(units, pad, gain_ref, gate_hbm, up_hbm, down_hbm, *refs):
    outs = refs[:SIDE]
    gate_ref, up_ref, down_ref, gate_t, up_t, sems = refs[SIDE:]
    waits = bring((gate_hbm, up_hbm, down_hbm), (gate_ref, up_ref, down_ref), sems)
    y = lax.axis_index("seq") % SIDE
    block = SIDE * units
    gain = gain_ref[...]
    for i, (source, target) in enumerate(((gate_ref, gate_t), (up_ref, up_t))):
        waits[i]()
        for c in range(source.shape[1] // HD):
            part = slice(c * HD, (c + 1) * HD)
            target[part] = source[:, part].astype(jnp.float32).T * gain
    waits[2]()
    zeros = jnp.zeros((pad - units, down_ref.shape[1]), jnp.float32)
    for k in range(SIDE):
        start = lax.rem(y + k, SIDE) * block
        at = pl.ds(pl.multiple_of(start, 8), block)
        gate, up = gate_t[at], up_t[at]
        down = down_ref[pl.ds(pl.multiple_of(start, 16), block)].astype(jnp.float32)
        rows = []
        for z in range(SIDE):
            part = slice(z * units, (z + 1) * units)
            rows += [gate[part], up[part]]
        for z in range(SIDE):
            rows += [down[z * units : (z + 1) * units], zeros]
        outs[k][...] = jnp.concatenate(rows, axis=0).astype(jnp.bfloat16)


def gate_up(units, hidden_ref, *refs):
    weights, out_ref = refs[:SIDE], refs[SIDE]
    y = lax.axis_index("seq") % SIDE
    total = None
    squares = None
    for k in range(SIDE):
        hidden = hidden_ref[lax.rem(y + SIDE - k, SIDE)]
        wide = hidden.astype(jnp.float32)
        term = dot_nt(weights[k][: 2 * SIDE * units], hidden)
        total = term if total is None else total + term
        squares = wide * wide if squares is None else squares + wide * wide
    row = jnp.sum(squares.T, axis=0, keepdims=True)
    extra = padded(parts_of(row, 2), EXTRA)
    for z in range(SIDE):
        own = total[2 * units * z : 2 * units * (z + 1)]
        out_ref[z] = jnp.concatenate([own, extra], axis=0).astype(jnp.bfloat16)


def activate(units, pad, got_ref, out_ref):
    sums = sum(got_ref[s].astype(jnp.float32) for s in range(SIDE))
    mean_square = (sums[2 * units : 2 * units + 1] + sums[2 * units + 1 : 2 * units + 2]) / D
    inverse = lax.rsqrt(mean_square + EPSILON)
    gate, up = sums[:units] * inverse, sums[units : 2 * units] * inverse
    activation = gate / (1.0 + jnp.exp(-gate)) * up
    zeros = jnp.zeros((pad - units, activation.shape[1]), jnp.float32)
    message = jnp.concatenate([activation, zeros], axis=0).astype(jnp.bfloat16)
    for i in range(SIDE):
        out_ref[i] = message


def down(units, act_ref, *refs):
    weights, out_ref = refs[:SIDE], refs[SIDE]
    y = lax.axis_index("seq") % SIDE
    pieces, pad, branches = act_ref.shape
    act = act_ref[...].reshape(pieces * pad, branches).T
    for k in range(SIDE):
        term = jnp.dot(act, weights[k][2 * SIDE * units :], preferred_element_type=jnp.float32)
        out_ref[lax.rem(y + SIDE - k, SIDE)] = term.astype(jnp.bfloat16)


def call(kernel, outs, name, *args, hbm=(), scratch=()):
    spec = lambda i: pl.BlockSpec(memory_space=pl.ANY if i in hbm else pltpu.VMEM)
    return pl.pallas_call(
        kernel,
        out_shape=outs,
        in_specs=[spec(i) for i in range(len(args))],
        scratch_shapes=scratch,
        compiler_params=pltpu.CompilerParams(vmem_limit_bytes=(56 if hbm else 32) * MIB),
        name=name,
    )(*args)


def exchange(x, groups):
    return lax.all_to_all(x, "seq", 0, 0, axis_index_groups=groups, tiled=True)


def kvh_sum(x, n):
    copies = jnp.broadcast_to(x.astype(jnp.bfloat16), (n,) + x.shape)
    got = lax.all_to_all(copies, "kvh", 0, 0, tiled=True)
    return jnp.sum(got.astype(jnp.float32), axis=0)


def on_device(n_kvh, queries, new_keys, new_values, prefix_keys, prefix_values, suffix_keys,
              suffix_values, prefix_offsets, suffix_lengths, out_weight, residual, norm_gain,
              w_gate, w_up, w_down):
    branches, width = residual.shape
    heads = queries.shape[1] // HD
    bands = SIDE
    band = branches // bands
    rows = heads * band
    hidden_units = w_gate.shape[1]
    units = hidden_units // SIDE**2
    pad = -(-units // 16) * 16
    bf16 = lambda *shape: jax.ShapeDtypeStruct(shape, jnp.bfloat16)
    like = lambda a: pltpu.VMEM(a.shape, a.dtype)
    copies_sem = lambda n: pltpu.SemaphoreType.DMA((n, PIECES))

    mine = call(
        functools.partial(arrange, units, pad),
        (bf16(SIDE * (2 * units + pad), width),) * SIDE,
        "arrange",
        norm_gain.reshape(1, width), w_gate, w_up, w_down,
        hbm=(1, 2, 3),
        scratch=[like(w_gate), like(w_up), like(w_down)]
        + [pltpu.VMEM((hidden_units, width), jnp.float32)] * 2 + [copies_sem(3)],
    )
    weights = [mine[0]]
    for k in range(1, SIDE):
        pairs = [(z * SIDE + y, z * SIDE + (y + k) % SIDE) for z in range(SIDE) for y in range(SIDE)]
        weights.append(lax.ppermute(mine[k], "seq", pairs))

    by_column = lambda a: jnp.tile(a.reshape(bands, band), (1, heads))
    message = call(
        functools.partial(attend, bands, band, heads),
        bf16(bands, rows + EXTRA, HD),
        "attend",
        by_column(prefix_offsets), by_column(suffix_lengths), queries, prefix_keys, prefix_values,
        suffix_keys, suffix_values,
        hbm=(3, 4, 5, 6),
        scratch=[like(prefix_keys), like(prefix_values), like(suffix_keys), like(suffix_values),
                 pltpu.VMEM((HD + EXTRA, prefix_keys.shape[0]), jnp.bfloat16), copies_sem(4)],
    )
    message = call(merge, bf16(SIDE, rows + EXTRA, HD), "merge", exchange(message, Z_GROUPS))
    own = call(
        functools.partial(finish, heads, band), bf16(SIDE, rows, HD), "finish",
        exchange(message, Y_GROUPS), queries, new_keys, new_values,
    )
    gathered = exchange(own, Z_GROUPS)
    attention = (
        gathered.reshape(bands, heads, band, HD).transpose(0, 2, 1, 3).reshape(branches, heads * HD)
    )

    projected = kvh_sum(jnp.dot(attention, out_weight, preferred_element_type=jnp.float32), n_kvh)
    hidden = (residual.astype(jnp.float32) + projected).astype(jnp.bfloat16)
    gathered = exchange(jnp.broadcast_to(hidden, (SIDE, branches, width)), Y_GROUPS)
    message = call(
        functools.partial(gate_up, units), bf16(SIDE, 2 * units + EXTRA, branches), "gate_up",
        gathered, *weights,
    )
    message = call(
        functools.partial(activate, units, pad), bf16(SIDE, pad, branches), "activate",
        exchange(message, Z_GROUPS),
    )
    message = call(
        functools.partial(down, units), bf16(SIDE, branches, width), "down",
        exchange(message, Z_GROUPS), *weights,
    )
    ffn_part = jnp.sum(exchange(message, Y_GROUPS).astype(jnp.float32), axis=0)
    mixed = (hidden.astype(jnp.float32) + kvh_sum(ffn_part, n_kvh)).astype(jnp.bfloat16)
    return (attention, mixed)


def solution(mesh):
    return jax.shard_map(
        functools.partial(on_device, mesh.shape["kvh"]),
        mesh=mesh,
        in_specs=(
            P(None, "kvh"),
            P(None, "kvh"),
            P(None, "kvh"),
            P("seq", "kvh"),
            P("seq", "kvh"),
            P(None, "seq", "kvh"),
            P(None, "seq", "kvh"),
            P(),
            P(),
            P("kvh", "seq"),
            P(None, "seq"),
            P("seq"),
            P("seq", "kvh"),
            P("seq", "kvh"),
            P("kvh", "seq"),
        ),
        out_specs=(P(None, "kvh"), P(None, "seq")),
        check_vma=False,
    )
```

```python
import functools
import math

import jax
import jax.numpy as jnp
from jax import lax
from jax.experimental import pallas as pl
from jax.experimental.pallas import tpu as pltpu
from jax.sharding import PartitionSpec as P

HD = 128
D = 8192
SIDE = 8
Z_GROUPS = [[z * SIDE + y for z in range(SIDE)] for y in range(SIDE)]
Y_GROUPS = [[z * SIDE + y for y in range(SIDE)] for z in range(SIDE)]
QUAD = 4
BLOCKS = SIDE * SIDE // QUAD


def seq_at(p, q):
    return (q // (SIDE // 2) * 2 + p // 2) * SIDE + q % (SIDE // 2) * 2 + p % 2


P_GROUPS = [[seq_at(p, q) for p in range(QUAD)] for q in range(BLOCKS)]
Q_GROUPS = [[seq_at(p, q) for q in range(BLOCKS)] for p in range(QUAD)]
NEG_FILL = -1e30
EPSILON = 1e-05
SCALE_LOG2 = math.log2(math.e) / math.sqrt(HD)
EXTRA = 16
PIECES = 4
MIB = 2**20


def dot_nt(a, b):
    return lax.dot_general(a, b, (((1,), (1,)), ((), ())), preferred_element_type=jnp.float32)


def parts_of(x, count):
    parts = []
    for _ in range(count):
        part = x.astype(jnp.bfloat16).astype(jnp.float32)
        parts.append(part)
        x = x - part
    return parts


def padded(rows, count):
    return jnp.concatenate(rows + [jnp.zeros_like(rows[0])] * (count - len(rows)), axis=0)


def with_ones(values):
    return jnp.concatenate([values.T, jnp.ones((EXTRA, values.shape[0]), values.dtype)], axis=0)


def bring(sources, targets, sems):
    waits = []
    for i, (source, target) in enumerate(zip(sources, targets)):
        size = source.shape[0] // PIECES
        copies = []
        for j in range(PIECES):
            part = pl.ds(j * size, size)
            copy = pltpu.make_async_copy(source.at[part], target.at[part], sems.at[i, j])
            copy.start()
            copies.append(copy)
        waits.append(lambda copies=copies: [copy.wait() for copy in copies])
    return waits


def own_place():
    seq = lax.axis_index("seq")
    return seq // SIDE % 2 * 2 + seq % 2


def head_rows(block, heads):
    return jnp.concatenate([block[:, h * HD : (h + 1) * HD] for h in range(heads)], axis=0)


def by_column(bands, band, numbers, shifts):
    size = numbers.shape[1]
    lane = lax.broadcasted_iota(jnp.int32, (bands, size), 1)
    mine = lane // band == lax.broadcasted_iota(jnp.int32, (bands, size), 0)
    digits = []
    for i, shift in enumerate(shifts):
        digit = lax.shift_right_logical(numbers, shift)
        if i > 0:
            digit = digit & 31
        digits.append(jnp.where(mine, digit.astype(jnp.float32), 0.0))
    row = lax.broadcasted_iota(jnp.int32, (size, size), 0)
    col = lax.broadcasted_iota(jnp.int32, (size, size), 1)
    spread = jnp.where(row % band == col % band, 1.0, 0.0).astype(jnp.bfloat16)
    got = jnp.dot(
        jnp.concatenate(digits, axis=0).astype(jnp.bfloat16), spread,
        preferred_element_type=jnp.float32,
    ).astype(jnp.int32)
    return sum(got[i * bands : (i + 1) * bands] << shift for i, shift in enumerate(shifts))


def attend(bands, band, heads, offsets_ref, lengths_ref, q_ref, k_hbm, v_hbm, sk_hbm, sv_hbm, out_ref,
           k_ref, v_ref, sk_ref, sv_ref, vt_ref, off_ref, len_ref, sems):
    context = k_ref.shape[0]
    tail = sk_ref.shape[1]
    cols = heads * band
    seq = lax.axis_index("seq")
    waits = bring((k_hbm, v_hbm, sk_hbm, sv_hbm), (k_ref, v_ref, sk_ref, sv_ref), sems)
    off_ref[...] = by_column(bands, band, offsets_ref[...], (10, 5, 0))
    len_ref[...] = by_column(bands, band, lengths_ref[...], (5, 0))
    waits[1]()
    vt_ref[...] = with_ones(v_ref[...])
    for i in (0, 2, 3):
        waits[i]()

    def queries_of(g):
        return head_rows(q_ref[pl.ds(pl.multiple_of(g * band, band), band), :], heads)

    def pair(p, carry):
        bases = (2 * p, 2 * p + 1)
        qs = [queries_of(g) for g in bases]
        both = jnp.concatenate(qs, axis=0)
        offset = jnp.concatenate([off_ref[pl.ds(g, 1), :] for g in bases], axis=1)
        scores = dot_nt(k_ref[...], both)
        pos = lax.broadcasted_iota(jnp.int32, scores.shape, 0)
        scores = jnp.where(pos < offset - seq * context, scores, NEG_FILL)
        peak = jnp.max(scores, axis=0, keepdims=True)
        tails = []
        for i, g in enumerate(bases):
            at = pl.multiple_of(g * band, band)
            keys = sk_ref[pl.ds(at, band)].reshape(band * tail, HD)
            tail_scores = dot_nt(keys, qs[i])
            row = lax.broadcasted_iota(jnp.int32, tail_scores.shape, 0)
            col = lax.broadcasted_iota(jnp.int32, tail_scores.shape, 1)
            length = len_ref[pl.ds(g, 1), :] - seq * tail
            live = (row // tail == col % band) & (row % tail < length)
            tails.append(jnp.where(live, tail_scores, NEG_FILL))
        tail_peak = jnp.concatenate([jnp.max(t, axis=0, keepdims=True) for t in tails], axis=1)
        peak = jnp.maximum(peak, tail_peak)
        weights = jnp.exp2((scores - peak) * SCALE_LOG2).astype(jnp.bfloat16)
        sums = jnp.dot(vt_ref[...], weights, preferred_element_type=jnp.float32)
        for i, g in enumerate(bases):
            at = pl.multiple_of(g * band, band)
            own = slice(i * cols, (i + 1) * cols)
            own_peak = peak[:, own]
            tail_weights = jnp.exp2((tails[i] - own_peak) * SCALE_LOG2).astype(jnp.bfloat16)
            values = with_ones(sv_ref[pl.ds(at, band)].reshape(band * tail, HD))
            full = sums[:, own] + jnp.dot(values, tail_weights, preferred_element_type=jnp.float32)
            some = own_peak > 0.5 * NEG_FILL
            total = jnp.where(some, full[HD : HD + 1], 0.0)
            output = jnp.where(some, full[:HD], 0.0).T
            stats = padded(parts_of(own_peak, 3) + parts_of(total, 2), EXTRA)
            out_ref[g] = jnp.concatenate([output, stats], axis=0).astype(jnp.bfloat16)
        return carry

    lax.fori_loop(0, bands // 2, pair, 0)


def merged(got_ref):
    count, rows = got_ref.shape[0], got_ref.shape[1] - EXTRA
    stats = [got_ref[s, rows:].astype(jnp.float32) for s in range(count)]
    peaks = [st[0:1] + st[1:2] + st[2:3] for st in stats]
    totals = [st[3:4] + st[4:5] for st in stats]
    peak = functools.reduce(jnp.maximum, peaks)
    factors = [jnp.exp2((p - peak) * SCALE_LOG2) for p in peaks]
    total = sum(f * t for f, t in zip(factors, totals))
    columns = padded(factors + [peak, total], rows).T
    output = sum(
        columns[:, s : s + 1] * got_ref[s, :rows].astype(jnp.float32) for s in range(count)
    )
    return output, peak, total, columns[:, count : count + 1], columns[:, count + 1 : count + 2]


def merge(got_ref, out_ref):
    output, peak, total, _, _ = merged(got_ref)
    stats = padded(parts_of(peak, 3) + parts_of(total, 2), EXTRA)
    message = jnp.concatenate([output, stats], axis=0).astype(jnp.bfloat16)
    for i in range(out_ref.shape[0]):
        out_ref[i] = message


def finish(heads, band, got_ref, q_ref, nk_ref, nv_ref, out_ref):
    output, _, _, peak, total = merged(got_ref)
    own = pl.ds(pl.multiple_of(lax.axis_index("seq") // SIDE * band, band), band)
    tiled = lambda ref: jnp.concatenate([ref[own, :].astype(jnp.float32)] * heads, axis=0)
    query = head_rows(q_ref[own, :], heads).astype(jnp.float32)
    fresh = jnp.sum(query * tiled(nk_ref), axis=1, keepdims=True)
    row_peak = jnp.maximum(peak, fresh)
    factor = jnp.exp2((peak - row_peak) * SCALE_LOG2)
    fresh_factor = jnp.exp2((fresh - row_peak) * SCALE_LOG2)
    numerator = factor * output + fresh_factor * tiled(nv_ref)
    attention = (numerator / (factor * total + fresh_factor)).astype(jnp.bfloat16)
    for i in range(out_ref.shape[0]):
        out_ref[i] = attention


def arrange(units, pad, gain_ref, gate_hbm, up_hbm, down_hbm, *refs):
    outs = refs[:QUAD]
    gate_ref, up_ref, down_ref, sems = refs[QUAD:]
    waits = bring((gate_hbm, up_hbm, down_hbm), (gate_ref, up_ref, down_ref), sems)
    place = own_place()
    block = BLOCKS * units
    gain = gain_ref[...]
    zeros = jnp.zeros((pad - units, down_ref.shape[1]), jnp.float32)
    for wait in waits:
        wait()
    for k in range(QUAD):
        target = place ^ k
        at = pl.ds(pl.multiple_of(target * block, math.gcd(block, HD)), block)
        gate, up = [ref[:, at].astype(jnp.float32).T * gain for ref in (gate_ref, up_ref)]
        rows = []
        for q in range(BLOCKS):
            part = slice(q * units, (q + 1) * units)
            rows += [gate[part], up[part]]
        size = 2 * block
        outs[k][:size] = jnp.concatenate(rows, axis=0).astype(jnp.bfloat16)
        at = pl.ds(pl.multiple_of(target * block, 16), block)
        down = down_ref[at].astype(jnp.float32)
        rows = []
        for q in range(BLOCKS):
            rows += [down[q * units : (q + 1) * units], zeros]
        outs[k][size:] = jnp.concatenate(rows, axis=0).astype(jnp.bfloat16)


def gate_up(units, hidden_ref, *refs):
    weights, out_ref = refs[:QUAD], refs[QUAD]
    place = own_place()
    total = None
    squares = None
    for k in range(QUAD):
        hidden = hidden_ref[place ^ k]
        wide = hidden.astype(jnp.float32)
        term = dot_nt(weights[k][: 2 * BLOCKS * units], hidden)
        total = term if total is None else total + term
        squares = wide * wide if squares is None else squares + wide * wide
    row = jnp.sum(squares.T, axis=0, keepdims=True)
    extra = padded(parts_of(row, 2), EXTRA)
    for q in range(BLOCKS):
        own = total[2 * units * q : 2 * units * (q + 1)]
        out_ref[q] = jnp.concatenate([own, extra], axis=0).astype(jnp.bfloat16)


def activate(units, pad, got_ref, out_ref):
    sums = sum(got_ref[q].astype(jnp.float32) for q in range(BLOCKS))
    mean_square = (sums[2 * units : 2 * units + 1] + sums[2 * units + 1 : 2 * units + 2]) / D
    inverse = lax.rsqrt(mean_square + EPSILON)
    gate, up = sums[:units] * inverse, sums[units : 2 * units] * inverse
    activation = gate / (1.0 + jnp.exp(-gate)) * up
    zeros = jnp.zeros((pad - units, activation.shape[1]), jnp.float32)
    message = jnp.concatenate([activation, zeros], axis=0).astype(jnp.bfloat16)
    for q in range(BLOCKS):
        out_ref[q] = message


def down(units, act_ref, *refs):
    weights, out_ref = refs[:QUAD], refs[QUAD]
    place = own_place()
    pieces, pad, branches = act_ref.shape
    act = act_ref[...].reshape(pieces * pad, branches).T
    for k in range(QUAD):
        term = jnp.dot(act, weights[k][2 * BLOCKS * units :], preferred_element_type=jnp.float32)
        out_ref[place ^ k] = term.astype(jnp.bfloat16)


def call(kernel, outs, name, *args, hbm=(), scratch=()):
    spec = lambda i: pl.BlockSpec(memory_space=pl.ANY if i in hbm else pltpu.VMEM)
    return pl.pallas_call(
        kernel,
        out_shape=outs,
        in_specs=[spec(i) for i in range(len(args))],
        scratch_shapes=scratch,
        compiler_params=pltpu.CompilerParams(vmem_limit_bytes=(56 if hbm else 32) * MIB),
        name=name,
    )(*args)


def exchange(x, groups):
    return lax.all_to_all(x, "seq", 0, 0, axis_index_groups=groups, tiled=True)


def gather(x, axis, count, groups=None):
    copies = jnp.broadcast_to(x, (count,) + x.shape)
    return lax.all_to_all(copies, axis, 0, 0, axis_index_groups=groups, tiled=True)


def kvh_sum(x, n):
    return jnp.sum(gather(x.astype(jnp.bfloat16), "kvh", n).astype(jnp.float32), axis=0)


def on_device(n_kvh, queries, new_keys, new_values, prefix_keys, prefix_values, suffix_keys,
              suffix_values, prefix_offsets, suffix_lengths, out_weight, residual, norm_gain,
              w_gate, w_up, w_down):
    branches, width = residual.shape
    heads = queries.shape[1] // HD
    bands = SIDE
    band = branches // bands
    rows = heads * band
    hidden_units = w_gate.shape[1]
    units = hidden_units // SIDE**2
    pad = -(-units // 16) * 16
    bf16 = lambda *shape: jax.ShapeDtypeStruct(shape, jnp.bfloat16)
    like = lambda a: pltpu.VMEM(a.shape, a.dtype)
    copies_sem = lambda n: pltpu.SemaphoreType.DMA((n, PIECES))

    message = call(
        functools.partial(attend, bands, band, heads),
        bf16(bands, rows + EXTRA, HD),
        "attend",
        prefix_offsets.reshape(1, branches), suffix_lengths.reshape(1, branches), queries,
        prefix_keys, prefix_values, suffix_keys, suffix_values,
        hbm=(3, 4, 5, 6),
        scratch=[like(prefix_keys), like(prefix_values), like(suffix_keys), like(suffix_values),
                 pltpu.VMEM((HD + EXTRA, prefix_keys.shape[0]), jnp.bfloat16),
                 pltpu.VMEM((bands, rows), jnp.int32), pltpu.VMEM((bands, rows), jnp.int32),
                 copies_sem(4)],
    )
    message, *moved = lax.optimization_barrier((message, w_gate, w_up, w_down))
    mine = call(
        functools.partial(arrange, units, pad),
        (bf16(BLOCKS * (2 * units + pad), width),) * QUAD,
        "arrange",
        norm_gain.reshape(1, width), *moved,
        hbm=(1, 2, 3),
        scratch=[like(w_gate), like(w_up), like(w_down), copies_sem(3)],
    )
    weights = [mine[0]]
    for k in range(1, QUAD):
        pairs = [(seq_at(p, q), seq_at(p ^ k, q)) for q in range(BLOCKS) for p in range(QUAD)]
        weights.append(lax.ppermute(mine[k], "seq", pairs))

    message = call(merge, bf16(SIDE, rows + EXTRA, HD), "merge", exchange(message, Z_GROUPS))
    own = call(
        functools.partial(finish, heads, band), bf16(SIDE, rows, HD), "finish",
        exchange(message, Y_GROUPS), queries, new_keys, new_values,
    )
    gathered = exchange(own, Z_GROUPS)
    gathered, *weights = lax.optimization_barrier((gathered, *weights))
    attention = (
        gathered.reshape(bands, heads, band, HD).transpose(0, 2, 1, 3).reshape(branches, heads * HD)
    )

    projected = kvh_sum(jnp.dot(attention, out_weight, preferred_element_type=jnp.float32), n_kvh)
    hidden = (residual.astype(jnp.float32) + projected).astype(jnp.bfloat16)
    message = call(
        functools.partial(gate_up, units), bf16(BLOCKS, 2 * units + EXTRA, branches), "gate_up",
        gather(hidden, "seq", QUAD, P_GROUPS), *weights,
    )
    message = call(
        functools.partial(activate, units, pad), bf16(BLOCKS, pad, branches), "activate",
        exchange(message, Q_GROUPS),
    )
    message = call(
        functools.partial(down, units), bf16(QUAD, branches, width), "down",
        exchange(message, Q_GROUPS), *weights,
    )
    ffn_part = jnp.sum(exchange(message, P_GROUPS).astype(jnp.float32), axis=0)
    mixed = (hidden.astype(jnp.float32) + kvh_sum(ffn_part, n_kvh)).astype(jnp.bfloat16)
    return (attention, mixed)


def solution(mesh):
    return jax.shard_map(
        functools.partial(on_device, mesh.shape["kvh"]),
        mesh=mesh,
        in_specs=(
            P(None, "kvh"),
            P(None, "kvh"),
            P(None, "kvh"),
            P("seq", "kvh"),
            P("seq", "kvh"),
            P(None, "seq", "kvh"),
            P(None, "seq", "kvh"),
            P(),
            P(),
            P("kvh", "seq"),
            P(None, "seq"),
            P("seq"),
            P("seq", "kvh"),
            P("seq", "kvh"),
            P("kvh", "seq"),
        ),
        out_specs=(P(None, "kvh"), P(None, "seq")),
        check_vma=False,
    )
```

```python
import functools
import math

import jax
import jax.numpy as jnp
from jax import lax
from jax.experimental import pallas as pl
from jax.experimental.pallas import tpu as pltpu
from jax.sharding import PartitionSpec as P

HD = 128
D = 8192
SIDE = 8
Z_GROUPS = [[z * SIDE + y for z in range(SIDE)] for y in range(SIDE)]
Y_GROUPS = [[z * SIDE + y for y in range(SIDE)] for z in range(SIDE)]
QUAD = 4
BLOCKS = SIDE * SIDE // QUAD


def seq_at(p, q):
    return (q // (SIDE // 2) * 2 + p // 2) * SIDE + q % (SIDE // 2) * 2 + p % 2


P_GROUPS = [[seq_at(p, q) for p in range(QUAD)] for q in range(BLOCKS)]
Q_GROUPS = [[seq_at(p, q) for q in range(BLOCKS)] for p in range(QUAD)]
NEG_FILL = -1e30
EPSILON = 1e-05
SCALE_LOG2 = math.log2(math.e) / math.sqrt(HD)
EXTRA = 16
PIECES = 4
MIB = 2**20


def dot_nt(a, b):
    return lax.dot_general(a, b, (((1,), (1,)), ((), ())), preferred_element_type=jnp.float32)


def parts_of(x, count):
    parts = []
    for _ in range(count):
        part = x.astype(jnp.bfloat16).astype(jnp.float32)
        parts.append(part)
        x = x - part
    return parts


def padded(rows, count):
    return jnp.concatenate(rows + [jnp.zeros_like(rows[0])] * (count - len(rows)), axis=0)


def with_ones(values):
    return jnp.concatenate([values.T, jnp.ones((EXTRA, values.shape[0]), values.dtype)], axis=0)


def bring(sources, targets, sems):
    waits = []
    for i, (source, target) in enumerate(zip(sources, targets)):
        size = source.shape[0] // PIECES
        copies = []
        for j in range(PIECES):
            part = pl.ds(j * size, size)
            copy = pltpu.make_async_copy(source.at[part], target.at[part], sems.at[i, j])
            copy.start()
            copies.append(copy)
        waits.append(lambda copies=copies: [copy.wait() for copy in copies])
    return waits


def own_place():
    seq = lax.axis_index("seq")
    return seq // SIDE % 2 * 2 + seq % 2


def head_rows(block, heads):
    return jnp.concatenate([block[:, h * HD : (h + 1) * HD] for h in range(heads)], axis=0)


def by_column(bands, band, numbers, shifts):
    size = numbers.shape[1]
    lane = lax.broadcasted_iota(jnp.int32, (bands, size), 1)
    mine = lane // band == lax.broadcasted_iota(jnp.int32, (bands, size), 0)
    digits = []
    for i, shift in enumerate(shifts):
        digit = lax.shift_right_logical(numbers, shift)
        if i > 0:
            digit = digit & 31
        digits.append(jnp.where(mine, digit.astype(jnp.float32), 0.0))
    row = lax.broadcasted_iota(jnp.int32, (size, size), 0)
    col = lax.broadcasted_iota(jnp.int32, (size, size), 1)
    spread = jnp.where(row % band == col % band, 1.0, 0.0).astype(jnp.bfloat16)
    got = jnp.dot(
        jnp.concatenate(digits, axis=0).astype(jnp.bfloat16), spread,
        preferred_element_type=jnp.float32,
    ).astype(jnp.int32)
    return sum(got[i * bands : (i + 1) * bands] << shift for i, shift in enumerate(shifts))


def attend(bands, band, heads, offsets_ref, lengths_ref, q_ref, k_hbm, v_hbm, sk_hbm, sv_hbm, out_ref,
           k_ref, v_ref, sk_ref, sv_ref, vt_ref, off_ref, len_ref, sems):
    context = k_ref.shape[0]
    tail = sk_ref.shape[1]
    cols = heads * band
    seq = lax.axis_index("seq")
    waits = bring((k_hbm, v_hbm, sk_hbm, sv_hbm), (k_ref, v_ref, sk_ref, sv_ref), sems)
    off_ref[...] = by_column(bands, band, offsets_ref[...], (10, 5, 0))
    len_ref[...] = by_column(bands, band, lengths_ref[...], (5, 0))

    def queries_of(g):
        return head_rows(q_ref[pl.ds(pl.multiple_of(g * band, band), band), :], heads)

    def pair(p, first):
        bases = (2 * p, 2 * p + 1)
        qs = [queries_of(g) for g in bases]
        both = jnp.concatenate(qs, axis=0)
        offset = jnp.concatenate([off_ref[pl.ds(g, 1), :] for g in bases], axis=1)
        if first:
            waits[0]()
        scores = dot_nt(k_ref[...], both)
        pos = lax.broadcasted_iota(jnp.int32, scores.shape, 0)
        scores = jnp.where(pos < offset - seq * context, scores, NEG_FILL)
        peak = jnp.max(scores, axis=0, keepdims=True)
        tails = []
        if first:
            waits[2]()
        for i, g in enumerate(bases):
            at = pl.multiple_of(g * band, band)
            keys = sk_ref[pl.ds(at, band)].reshape(band * tail, HD)
            tail_scores = dot_nt(keys, qs[i])
            row = lax.broadcasted_iota(jnp.int32, tail_scores.shape, 0)
            col = lax.broadcasted_iota(jnp.int32, tail_scores.shape, 1)
            length = len_ref[pl.ds(g, 1), :] - seq * tail
            live = (row // tail == col % band) & (row % tail < length)
            tails.append(jnp.where(live, tail_scores, NEG_FILL))
        tail_peak = jnp.concatenate([jnp.max(t, axis=0, keepdims=True) for t in tails], axis=1)
        peak = jnp.maximum(peak, tail_peak)
        weights = jnp.exp2((scores - peak) * SCALE_LOG2).astype(jnp.bfloat16)
        if first:
            waits[1]()
            vt_ref[...] = with_ones(v_ref[...])
            waits[3]()
        sums = jnp.dot(vt_ref[...], weights, preferred_element_type=jnp.float32)
        for i, g in enumerate(bases):
            at = pl.multiple_of(g * band, band)
            own = slice(i * cols, (i + 1) * cols)
            own_peak = peak[:, own]
            tail_weights = jnp.exp2((tails[i] - own_peak) * SCALE_LOG2).astype(jnp.bfloat16)
            values = with_ones(sv_ref[pl.ds(at, band)].reshape(band * tail, HD))
            full = sums[:, own] + jnp.dot(values, tail_weights, preferred_element_type=jnp.float32)
            some = own_peak > 0.5 * NEG_FILL
            total = jnp.where(some, full[HD : HD + 1], 0.0)
            output = jnp.where(some, full[:HD], 0.0).T
            stats = padded(parts_of(own_peak, 3) + parts_of(total, 2), EXTRA)
            out_ref[g] = jnp.concatenate([output, stats], axis=0).astype(jnp.bfloat16)

    pair(0, True)
    pl.loop(1, bands // 2)(lambda p: pair(p, False))


def merged(got_ref):
    count, rows = got_ref.shape[0], got_ref.shape[1] - EXTRA
    stats = [got_ref[s, rows:].astype(jnp.float32) for s in range(count)]
    peaks = [st[0:1] + st[1:2] + st[2:3] for st in stats]
    totals = [st[3:4] + st[4:5] for st in stats]
    peak = functools.reduce(jnp.maximum, peaks)
    factors = [jnp.exp2((p - peak) * SCALE_LOG2) for p in peaks]
    total = sum(f * t for f, t in zip(factors, totals))
    columns = padded(factors + [peak, total], rows).T
    output = sum(
        columns[:, s : s + 1] * got_ref[s, :rows].astype(jnp.float32) for s in range(count)
    )
    return output, peak, total, columns[:, count : count + 1], columns[:, count + 1 : count + 2]


def merge(got_ref, out_ref):
    output, peak, total, _, _ = merged(got_ref)
    stats = padded(parts_of(peak, 3) + parts_of(total, 2), EXTRA)
    message = jnp.concatenate([output, stats], axis=0).astype(jnp.bfloat16)
    for i in range(out_ref.shape[0]):
        out_ref[i] = message


def finish(heads, band, got_ref, q_ref, nk_ref, nv_ref, out_ref):
    output, _, _, peak, total = merged(got_ref)
    own = pl.ds(pl.multiple_of(lax.axis_index("seq") // SIDE * band, band), band)
    tiled = lambda ref: jnp.concatenate([ref[own, :].astype(jnp.float32)] * heads, axis=0)
    query = head_rows(q_ref[own, :], heads).astype(jnp.float32)
    fresh = jnp.sum(query * tiled(nk_ref), axis=1, keepdims=True)
    row_peak = jnp.maximum(peak, fresh)
    factor = jnp.exp2((peak - row_peak) * SCALE_LOG2)
    fresh_factor = jnp.exp2((fresh - row_peak) * SCALE_LOG2)
    numerator = factor * output + fresh_factor * tiled(nv_ref)
    attention = (numerator / (factor * total + fresh_factor)).astype(jnp.bfloat16)
    for i in range(out_ref.shape[0]):
        out_ref[i] = attention


def arrange(gate_hbm, up_hbm, down_hbm, *refs):
    both, downs, sems = refs[:QUAD], refs[QUAD : 2 * QUAD], refs[2 * QUAD]
    block = down_hbm.shape[0] // QUAD
    copies = []
    for k in range(QUAD):
        start = (own_place() ^ k) * block
        columns = pl.ds(pl.multiple_of(start, HD), block)
        rows = pl.ds(pl.multiple_of(start, 16), block)
        pairs = (
            (gate_hbm.at[:, columns], both[k].at[0]),
            (up_hbm.at[:, columns], both[k].at[1]),
            (down_hbm.at[rows], downs[k]),
        )
        for i, (source, target) in enumerate(pairs):
            copies.append(pltpu.make_async_copy(source, target, sems.at[k, i]))
            copies[-1].start()
    for copy in copies:
        copy.wait()


def combine(got_ref, residual_ref, gain_ref, hidden_ref, out_ref):
    projected = sum(got_ref[k].astype(jnp.float32) for k in range(got_ref.shape[0]))
    hidden = (residual_ref[...].astype(jnp.float32) + projected).astype(jnp.bfloat16)
    hidden_ref[...] = hidden
    wide = hidden.astype(jnp.float32)
    squares = jnp.sum((wide * wide).T, axis=0, keepdims=True)
    message = jnp.concatenate(
        [wide * gain_ref[...], padded(parts_of(squares, 2), EXTRA)], axis=0
    ).astype(jnp.bfloat16)
    for p in range(QUAD):
        out_ref[p] = message


def gate_up(units, hidden_ref, *refs):
    weights, out_ref = refs[:QUAD], refs[QUAD]
    place = own_place()
    rows = hidden_ref.shape[1] - EXTRA
    totals = [None, None]
    squares = None
    for k in range(QUAD):
        message = hidden_ref[place ^ k]
        hidden = message[:rows]
        extra = message[rows:].astype(jnp.float32)
        row = extra[0:1] + extra[1:2]
        squares = row if squares is None else squares + row
        for i in range(2):
            term = jnp.dot(hidden, weights[k][i], preferred_element_type=jnp.float32)
            totals[i] = term if totals[i] is None else totals[i] + term
    gate, up = [total.T for total in totals]
    extra = padded(parts_of(squares, 2), EXTRA)
    for q in range(BLOCKS):
        part = slice(units * q, units * (q + 1))
        out_ref[q] = jnp.concatenate([gate[part], up[part], extra], axis=0).astype(jnp.bfloat16)


def activate(units, pad, got_ref, out_ref):
    sums = sum(got_ref[q].astype(jnp.float32) for q in range(BLOCKS))
    mean_square = (sums[2 * units : 2 * units + 1] + sums[2 * units + 1 : 2 * units + 2]) / D
    inverse = lax.rsqrt(mean_square + EPSILON)
    gate, up = sums[:units] * inverse, sums[units : 2 * units] * inverse
    activation = gate / (1.0 + jnp.exp(-gate)) * up
    zeros = jnp.zeros((pad - units, activation.shape[1]), jnp.float32)
    message = jnp.concatenate([activation, zeros], axis=0).astype(jnp.bfloat16)
    for q in range(BLOCKS):
        out_ref[q] = message


def down(units, act_ref, *refs):
    weights, out_ref = refs[:QUAD], refs[QUAD]
    place = own_place()
    rows = [act_ref[q].astype(jnp.float32)[:units] for q in range(BLOCKS)]
    act = jnp.concatenate(rows, axis=0).T.astype(jnp.bfloat16)
    for k in range(QUAD):
        term = jnp.dot(act, weights[k][...], preferred_element_type=jnp.float32)
        out_ref[place ^ k] = term.astype(jnp.bfloat16)


def call(kernel, outs, name, *args, hbm=(), scratch=(), out_memory=pltpu.VMEM):
    spec = lambda i: pl.BlockSpec(memory_space=pl.ANY if i in hbm else pltpu.VMEM)
    return pl.pallas_call(
        kernel,
        out_shape=outs,
        in_specs=[spec(i) for i in range(len(args))],
        out_specs=jax.tree.map(lambda _: pl.BlockSpec(memory_space=out_memory), outs),
        scratch_shapes=scratch,
        compiler_params=pltpu.CompilerParams(vmem_limit_bytes=(56 if hbm else 32) * MIB),
        name=name,
    )(*args)


def exchange(x, groups):
    return lax.all_to_all(x, "seq", 0, 0, axis_index_groups=groups, tiled=True)


def gather(x, axis, count, groups=None):
    copies = jnp.broadcast_to(x, (count,) + x.shape)
    return lax.all_to_all(copies, axis, 0, 0, axis_index_groups=groups, tiled=True)


def on_device(n_kvh, queries, new_keys, new_values, prefix_keys, prefix_values, suffix_keys,
              suffix_values, prefix_offsets, suffix_lengths, out_weight, residual, norm_gain,
              w_gate, w_up, w_down):
    branches, width = residual.shape
    heads = queries.shape[1] // HD
    bands = SIDE
    band = branches // bands
    rows = heads * band
    hidden_units = w_gate.shape[1]
    units = hidden_units // SIDE**2
    pad = -(-units // 16) * 16
    bf16 = lambda *shape: jax.ShapeDtypeStruct(shape, jnp.bfloat16)
    like = lambda a: pltpu.VMEM(a.shape, a.dtype)
    copies_sem = lambda n: pltpu.SemaphoreType.DMA((n, PIECES))

    message = call(
        functools.partial(attend, bands, band, heads),
        bf16(bands, rows + EXTRA, HD),
        "attend",
        prefix_offsets.reshape(1, branches), suffix_lengths.reshape(1, branches), queries,
        prefix_keys, prefix_values, suffix_keys, suffix_values,
        hbm=(3, 4, 5, 6),
        scratch=[like(prefix_keys), like(prefix_values), like(suffix_keys), like(suffix_values),
                 pltpu.VMEM((HD + EXTRA, prefix_keys.shape[0]), jnp.bfloat16),
                 pltpu.VMEM((bands, rows), jnp.int32), pltpu.VMEM((bands, rows), jnp.int32),
                 copies_sem(4)],
    )
    message, *moved = lax.optimization_barrier((message, w_gate, w_up, w_down))
    block = hidden_units // QUAD
    mine = call(
        arrange,
        (bf16(2, width, block),) * QUAD + (bf16(block, width),) * QUAD,
        "arrange",
        *moved,
        hbm=(0, 1, 2),
        out_memory=pl.ANY,
        scratch=[pltpu.SemaphoreType.DMA((QUAD, 3))],
    )
    swap = lambda x, k: lax.ppermute(
        x, "seq", [(seq_at(p, q), seq_at(p ^ k, q)) for q in range(BLOCKS) for p in range(QUAD)]
    )
    both = [mine[0]] + [swap(mine[k], k) for k in range(1, QUAD)]

    message = call(merge, bf16(SIDE, rows + EXTRA, HD), "merge", exchange(message, Z_GROUPS))
    message, *downs = lax.optimization_barrier((message, *mine[QUAD:]))
    downs = downs[:1] + [swap(downs[k], k) for k in range(1, QUAD)]
    own = call(
        functools.partial(finish, heads, band), bf16(SIDE, rows, HD), "finish",
        exchange(message, Y_GROUPS), queries, new_keys, new_values,
    )
    own, *both = lax.optimization_barrier((own, *both))
    gathered = exchange(own, Z_GROUPS)
    attention = (
        gathered.reshape(bands, heads, band, HD).transpose(0, 2, 1, 3).reshape(branches, heads * HD)
    )

    projected = jnp.dot(attention, out_weight, preferred_element_type=jnp.float32)
    hidden, message = call(
        combine, (bf16(branches, width), bf16(QUAD, branches + EXTRA, width)), "combine",
        gather(projected.astype(jnp.bfloat16), "kvh", n_kvh), residual, norm_gain.reshape(1, width),
    )
    message, *downs = lax.optimization_barrier((message, *downs))
    message = call(
        functools.partial(gate_up, units), bf16(BLOCKS, 2 * units + EXTRA, branches), "gate_up",
        exchange(message, P_GROUPS), *both,
    )
    message = call(
        functools.partial(activate, units, pad), bf16(BLOCKS, pad, branches), "activate",
        exchange(message, Q_GROUPS),
    )
    message = call(
        functools.partial(down, units), bf16(QUAD, branches, width), "down",
        exchange(message, Q_GROUPS), *downs,
    )
    ffn_part = jnp.sum(exchange(message, P_GROUPS).astype(jnp.float32), axis=0)
    terms = gather(ffn_part.astype(jnp.bfloat16), "kvh", n_kvh)
    ffn_sum = jnp.sum(terms.astype(jnp.float32), axis=0)
    mixed = (hidden.astype(jnp.float32) + ffn_sum).astype(jnp.bfloat16)
    return (attention, mixed)


def solution(mesh):
    return jax.shard_map(
        functools.partial(on_device, mesh.shape["kvh"]),
        mesh=mesh,
        in_specs=(
            P(None, "kvh"),
            P(None, "kvh"),
            P(None, "kvh"),
            P("seq", "kvh"),
            P("seq", "kvh"),
            P(None, "seq", "kvh"),
            P(None, "seq", "kvh"),
            P(),
            P(),
            P("kvh", "seq"),
            P(None, "seq"),
            P("seq"),
            P("seq", "kvh"),
            P("seq", "kvh"),
            P("kvh", "seq"),
        ),
        out_specs=(P(None, "kvh"), P(None, "seq")),
        check_vma=False,
    )
```

```python
import functools
import math

import jax
import jax.numpy as jnp
from jax import lax
from jax.experimental import pallas as pl
from jax.experimental.pallas import tpu as pltpu
from jax.sharding import PartitionSpec as P

HD = 128
D = 8192
SIDE = 8
Z_GROUPS = [[z * SIDE + y for z in range(SIDE)] for y in range(SIDE)]
Y_GROUPS = [[z * SIDE + y for y in range(SIDE)] for z in range(SIDE)]
QUAD = 4
BLOCKS = SIDE * SIDE // QUAD


def seq_at(p, q):
    return (q // (SIDE // 2) * 2 + p // 2) * SIDE + q % (SIDE // 2) * 2 + p % 2


P_GROUPS = [[seq_at(p, q) for p in range(QUAD)] for q in range(BLOCKS)]
Q_GROUPS = [[seq_at(p, q) for q in range(BLOCKS)] for p in range(QUAD)]
NEG_FILL = -1e30
EPSILON = 1e-05
SCALE_LOG2 = math.log2(math.e) / math.sqrt(HD)
EXTRA = 16
PIECES = 4
MIB = 2**20


def dot_nt(a, b):
    return lax.dot_general(a, b, (((1,), (1,)), ((), ())), preferred_element_type=jnp.float32)


def parts_of(x, count):
    parts = []
    for _ in range(count):
        part = x.astype(jnp.bfloat16).astype(jnp.float32)
        parts.append(part)
        x = x - part
    return parts


def padded(rows, count):
    return jnp.concatenate(rows + [jnp.zeros_like(rows[0])] * (count - len(rows)), axis=0)


def with_ones(values):
    return jnp.concatenate([values.T, jnp.ones((EXTRA, values.shape[0]), values.dtype)], axis=0)


def bring(sources, targets, sems):
    waits = []
    for i, (source, target) in enumerate(zip(sources, targets)):
        size = source.shape[0] // PIECES
        copies = []
        for j in range(PIECES):
            part = pl.ds(j * size, size)
            copy = pltpu.make_async_copy(source.at[part], target.at[part], sems.at[i, j])
            copy.start()
            copies.append(copy)
        waits.append(lambda copies=copies: [copy.wait() for copy in copies])
    return waits


def own_place():
    seq = lax.axis_index("seq")
    return seq // SIDE % 2 * 2 + seq % 2


def head_rows(block, heads):
    return jnp.concatenate([block[:, h * HD : (h + 1) * HD] for h in range(heads)], axis=0)


def by_column(bands, band, numbers, shifts):
    size = numbers.shape[1]
    lane = lax.broadcasted_iota(jnp.int32, (bands, size), 1)
    mine = lane // band == lax.broadcasted_iota(jnp.int32, (bands, size), 0)
    digits = []
    for i, shift in enumerate(shifts):
        digit = lax.shift_right_logical(numbers, shift)
        if i > 0:
            digit = digit & 31
        digits.append(jnp.where(mine, digit.astype(jnp.float32), 0.0))
    row = lax.broadcasted_iota(jnp.int32, (size, size), 0)
    col = lax.broadcasted_iota(jnp.int32, (size, size), 1)
    spread = jnp.where(row % band == col % band, 1.0, 0.0).astype(jnp.bfloat16)
    got = jnp.dot(
        jnp.concatenate(digits, axis=0).astype(jnp.bfloat16), spread,
        preferred_element_type=jnp.float32,
    ).astype(jnp.int32)
    return sum(got[i * bands : (i + 1) * bands] << shift for i, shift in enumerate(shifts))


def attend(bands, band, heads, offsets_ref, lengths_ref, q_hbm, k_hbm, v_hbm, sk_hbm, sv_hbm, out_ref,
           q_ref, k_ref, v_ref, sk_ref, sv_ref, vt_ref, off_ref, len_ref, sems):
    context = k_ref.shape[0]
    tail = sk_ref.shape[1]
    cols = heads * band
    seq = lax.axis_index("seq")
    waits = bring(
        (q_hbm, k_hbm, sk_hbm, v_hbm, sv_hbm), (q_ref, k_ref, sk_ref, v_ref, sv_ref), sems
    )
    off_ref[...] = by_column(bands, band, offsets_ref[...], (10, 5, 0))
    len_ref[...] = by_column(bands, band, lengths_ref[...], (5, 0))

    def queries_of(g):
        return head_rows(q_ref[pl.ds(pl.multiple_of(g * band, band), band), :], heads)

    def pair(p, first):
        bases = (2 * p, 2 * p + 1)
        if first:
            waits[0]()
        qs = [queries_of(g) for g in bases]
        both = jnp.concatenate(qs, axis=0)
        offset = jnp.concatenate([off_ref[pl.ds(g, 1), :] for g in bases], axis=1)
        if first:
            waits[1]()
        scores = dot_nt(k_ref[...], both)
        pos = lax.broadcasted_iota(jnp.int32, scores.shape, 0)
        scores = jnp.where(pos < offset - seq * context, scores, NEG_FILL)
        peak = jnp.max(scores, axis=0, keepdims=True)
        tails = []
        if first:
            waits[2]()
        for i, g in enumerate(bases):
            at = pl.multiple_of(g * band, band)
            keys = sk_ref[pl.ds(at, band)].reshape(band * tail, HD)
            tail_scores = dot_nt(keys, qs[i])
            row = lax.broadcasted_iota(jnp.int32, tail_scores.shape, 0)
            col = lax.broadcasted_iota(jnp.int32, tail_scores.shape, 1)
            length = len_ref[pl.ds(g, 1), :] - seq * tail
            live = (row // tail == col % band) & (row % tail < length)
            tails.append(jnp.where(live, tail_scores, NEG_FILL))
        tail_peak = jnp.concatenate([jnp.max(t, axis=0, keepdims=True) for t in tails], axis=1)
        peak = jnp.maximum(peak, tail_peak)
        weights = jnp.exp2((scores - peak) * SCALE_LOG2).astype(jnp.bfloat16)
        if first:
            waits[3]()
            vt_ref[...] = with_ones(v_ref[...])
            waits[4]()
        sums = jnp.dot(vt_ref[...], weights, preferred_element_type=jnp.float32)
        for i, g in enumerate(bases):
            at = pl.multiple_of(g * band, band)
            own = slice(i * cols, (i + 1) * cols)
            own_peak = peak[:, own]
            tail_weights = jnp.exp2((tails[i] - own_peak) * SCALE_LOG2).astype(jnp.bfloat16)
            values = with_ones(sv_ref[pl.ds(at, band)].reshape(band * tail, HD))
            full = sums[:, own] + jnp.dot(values, tail_weights, preferred_element_type=jnp.float32)
            some = own_peak > 0.5 * NEG_FILL
            total = jnp.where(some, full[HD : HD + 1], 0.0)
            output = jnp.where(some, full[:HD], 0.0).T
            stats = padded(parts_of(own_peak, 3) + parts_of(total, 2), EXTRA)
            out_ref[g] = jnp.concatenate([output, stats], axis=0).astype(jnp.bfloat16)

    pair(0, True)
    pl.loop(1, bands // 2)(lambda p: pair(p, False))


def merged(got_ref):
    count, rows = got_ref.shape[0], got_ref.shape[1] - EXTRA
    stats = [got_ref[s, rows:].astype(jnp.float32) for s in range(count)]
    peaks = [st[0:1] + st[1:2] + st[2:3] for st in stats]
    totals = [st[3:4] + st[4:5] for st in stats]
    peak = functools.reduce(jnp.maximum, peaks)
    factors = [jnp.exp2((p - peak) * SCALE_LOG2) for p in peaks]
    total = sum(f * t for f, t in zip(factors, totals))
    columns = padded(factors + [peak, total], rows).T
    output = sum(
        columns[:, s : s + 1] * got_ref[s, :rows].astype(jnp.float32) for s in range(count)
    )
    return output, peak, total, columns[:, count : count + 1], columns[:, count + 1 : count + 2]


def merge(got_ref, out_ref):
    output, peak, total, _, _ = merged(got_ref)
    stats = padded(parts_of(peak, 3) + parts_of(total, 2), EXTRA)
    message = jnp.concatenate([output, stats], axis=0).astype(jnp.bfloat16)
    for i in range(out_ref.shape[0]):
        out_ref[i] = message


def finish(heads, band, got_ref, q_ref, nk_ref, nv_ref, out_ref):
    output, _, _, peak, total = merged(got_ref)
    own = pl.ds(pl.multiple_of(lax.axis_index("seq") // SIDE * band, band), band)
    tiled = lambda ref: jnp.concatenate([ref[own, :].astype(jnp.float32)] * heads, axis=0)
    query = head_rows(q_ref[own, :], heads).astype(jnp.float32)
    fresh = jnp.sum(query * tiled(nk_ref), axis=1, keepdims=True)
    row_peak = jnp.maximum(peak, fresh)
    factor = jnp.exp2((peak - row_peak) * SCALE_LOG2)
    fresh_factor = jnp.exp2((fresh - row_peak) * SCALE_LOG2)
    numerator = factor * output + fresh_factor * tiled(nv_ref)
    attention = (numerator / (factor * total + fresh_factor)).astype(jnp.bfloat16)
    for i in range(out_ref.shape[0]):
        out_ref[i] = attention


def arrange(gate_ref, up_ref, *outs):
    block = outs[0].shape[2]
    for k in range(QUAD):
        columns = pl.ds(pl.multiple_of((own_place() ^ k) * block, HD), block)
        outs[k][0] = gate_ref[:, columns]
        outs[k][1] = up_ref[:, columns]


def combine(got_ref, residual_ref, gain_ref, hidden_ref, out_ref):
    projected = sum(got_ref[k].astype(jnp.float32) for k in range(got_ref.shape[0]))
    hidden = (residual_ref[...].astype(jnp.float32) + projected).astype(jnp.bfloat16)
    hidden_ref[...] = hidden
    wide = hidden.astype(jnp.float32)
    squares = jnp.sum((wide * wide).T, axis=0, keepdims=True)
    message = jnp.concatenate(
        [wide * gain_ref[...], padded(parts_of(squares, 2), EXTRA)], axis=0
    ).astype(jnp.bfloat16)
    for p in range(QUAD):
        out_ref[p] = message


def gate_up(units, hidden_ref, *refs):
    weights, out_ref = refs[:QUAD], refs[QUAD]
    place = own_place()
    rows = hidden_ref.shape[1] - EXTRA
    totals = [None, None]
    squares = None
    for k in range(QUAD):
        message = hidden_ref[place ^ k]
        hidden = message[:rows]
        extra = message[rows:].astype(jnp.float32)
        row = extra[0:1] + extra[1:2]
        squares = row if squares is None else squares + row
        for i in range(2):
            term = jnp.dot(hidden, weights[k][i], preferred_element_type=jnp.float32)
            totals[i] = term if totals[i] is None else totals[i] + term
    gate, up = [total.T for total in totals]
    extra = padded(parts_of(squares, 2), EXTRA)
    for q in range(BLOCKS):
        part = slice(units * q, units * (q + 1))
        out_ref[q] = jnp.concatenate([gate[part], up[part], extra], axis=0).astype(jnp.bfloat16)


def activate(units, pad, got_ref, out_ref):
    sums = sum(got_ref[q].astype(jnp.float32) for q in range(BLOCKS))
    mean_square = (sums[2 * units : 2 * units + 1] + sums[2 * units + 1 : 2 * units + 2]) / D
    inverse = lax.rsqrt(mean_square + EPSILON)
    gate, up = sums[:units] * inverse, sums[units : 2 * units] * inverse
    activation = gate / (1.0 + jnp.exp(-gate)) * up
    zeros = jnp.zeros((pad - units, activation.shape[1]), jnp.float32)
    message = jnp.concatenate([activation, zeros], axis=0).astype(jnp.bfloat16)
    for q in range(BLOCKS):
        out_ref[q] = message


def down(units, act_ref, *refs):
    weights, out_ref = refs[:QUAD], refs[QUAD]
    place = own_place()
    rows = [act_ref[q].astype(jnp.float32)[:units] for q in range(BLOCKS)]
    act = jnp.concatenate(rows, axis=0).T.astype(jnp.bfloat16)
    for k in range(QUAD):
        term = jnp.dot(act, weights[k][...], preferred_element_type=jnp.float32)
        out_ref[place ^ k] = term.astype(jnp.bfloat16)


def call(kernel, outs, name, *args, hbm=(), scratch=()):
    spec = lambda i: pl.BlockSpec(memory_space=pl.ANY if i in hbm else pltpu.VMEM)
    return pl.pallas_call(
        kernel,
        out_shape=outs,
        in_specs=[spec(i) for i in range(len(args))],
        scratch_shapes=scratch,
        compiler_params=pltpu.CompilerParams(vmem_limit_bytes=(56 if hbm else 32) * MIB),
        name=name,
    )(*args)


def exchange(x, groups):
    return lax.all_to_all(x, "seq", 0, 0, axis_index_groups=groups, tiled=True)


def gather(x, axis, count, groups=None):
    copies = jnp.broadcast_to(x, (count,) + x.shape)
    return lax.all_to_all(copies, axis, 0, 0, axis_index_groups=groups, tiled=True)


def on_device(n_kvh, queries, new_keys, new_values, prefix_keys, prefix_values, suffix_keys,
              suffix_values, prefix_offsets, suffix_lengths, out_weight, residual, norm_gain,
              w_gate, w_up, w_down):
    branches, width = residual.shape
    heads = queries.shape[1] // HD
    bands = SIDE
    band = branches // bands
    rows = heads * band
    hidden_units = w_gate.shape[1]
    units = hidden_units // SIDE**2
    pad = -(-units // 16) * 16
    bf16 = lambda *shape: jax.ShapeDtypeStruct(shape, jnp.bfloat16)
    like = lambda a: pltpu.VMEM(a.shape, a.dtype)
    copies_sem = lambda n: pltpu.SemaphoreType.DMA((n, PIECES))

    message = call(
        functools.partial(attend, bands, band, heads),
        bf16(bands, rows + EXTRA, HD),
        "attend",
        prefix_offsets.reshape(1, branches), suffix_lengths.reshape(1, branches), queries,
        prefix_keys, prefix_values, suffix_keys, suffix_values,
        hbm=(2, 3, 4, 5, 6),
        scratch=[like(queries), like(prefix_keys), like(prefix_values), like(suffix_keys),
                 like(suffix_values),
                 pltpu.VMEM((HD + EXTRA, prefix_keys.shape[0]), jnp.bfloat16),
                 pltpu.VMEM((bands, rows), jnp.int32), pltpu.VMEM((bands, rows), jnp.int32),
                 copies_sem(5)],
    )
    message, *moved = lax.optimization_barrier((message, w_gate, w_up))
    block = hidden_units // QUAD
    mine = call(arrange, (bf16(2, width, block),) * QUAD, "arrange", *moved)
    swap = lambda x, k: lax.ppermute(
        x, "seq", [(seq_at(p, q), seq_at(p ^ k, q)) for q in range(BLOCKS) for p in range(QUAD)]
    )
    both = [mine[0]] + [swap(mine[k], k) for k in range(1, QUAD)]

    message = call(merge, bf16(SIDE, rows + EXTRA, HD), "merge", exchange(message, Z_GROUPS))
    own = call(
        functools.partial(finish, heads, band), bf16(SIDE, rows, HD), "finish",
        exchange(message, Y_GROUPS), queries, new_keys, new_values,
    )
    gathered = exchange(own, Z_GROUPS)
    gathered, *both = lax.optimization_barrier((gathered, *both))
    attention = (
        gathered.reshape(bands, heads, band, HD).transpose(0, 2, 1, 3).reshape(branches, heads * HD)
    )

    projected = jnp.dot(attention, out_weight, preferred_element_type=jnp.float32)
    hidden, message = call(
        combine, (bf16(branches, width), bf16(QUAD, branches + EXTRA, width)), "combine",
        gather(projected.astype(jnp.bfloat16), "kvh", n_kvh), residual, norm_gain.reshape(1, width),
    )
    message, moved = lax.optimization_barrier((message, w_down))
    downs = [
        lax.dynamic_slice_in_dim(moved, (own_place() ^ k) * block, block) for k in range(QUAD)
    ]
    downs = downs[:1] + [swap(downs[k], k) for k in range(1, QUAD)]
    message = call(
        functools.partial(gate_up, units), bf16(BLOCKS, 2 * units + EXTRA, branches), "gate_up",
        exchange(message, P_GROUPS), *both,
    )
    message = call(
        functools.partial(activate, units, pad), bf16(BLOCKS, pad, branches), "activate",
        exchange(message, Q_GROUPS),
    )
    message, *downs = lax.optimization_barrier((message, *downs))
    message = call(
        functools.partial(down, units), bf16(QUAD, branches, width), "down",
        exchange(message, Q_GROUPS), *downs,
    )
    ffn_part = jnp.sum(exchange(message, P_GROUPS).astype(jnp.float32), axis=0)
    terms = gather(ffn_part.astype(jnp.bfloat16), "kvh", n_kvh)
    ffn_sum = jnp.sum(terms.astype(jnp.float32), axis=0)
    mixed = (hidden.astype(jnp.float32) + ffn_sum).astype(jnp.bfloat16)
    return (attention, mixed)


def solution(mesh):
    return jax.shard_map(
        functools.partial(on_device, mesh.shape["kvh"]),
        mesh=mesh,
        in_specs=(
            P(None, "kvh"),
            P(None, "kvh"),
            P(None, "kvh"),
            P("seq", "kvh"),
            P("seq", "kvh"),
            P(None, "seq", "kvh"),
            P(None, "seq", "kvh"),
            P(),
            P(),
            P("kvh", "seq"),
            P(None, "seq"),
            P("seq"),
            P("seq", "kvh"),
            P("seq", "kvh"),
            P("kvh", "seq"),
        ),
        out_specs=(P(None, "kvh"), P(None, "seq")),
        check_vma=False,
    )
```

```python
import functools
import math

import jax
import jax.numpy as jnp
from jax import lax
from jax.experimental import pallas as pl
from jax.experimental.pallas import tpu as pltpu
from jax.sharding import PartitionSpec as P

HD = 128
D = 8192
SIDE = 8
Z_GROUPS = [[z * SIDE + y for z in range(SIDE)] for y in range(SIDE)]
Y_GROUPS = [[z * SIDE + y for y in range(SIDE)] for z in range(SIDE)]
QUAD = 4
BLOCKS = SIDE * SIDE // QUAD


def seq_at(p, q):
    return (q // (SIDE // 2) * 2 + p // 2) * SIDE + q % (SIDE // 2) * 2 + p % 2


P_GROUPS = [[seq_at(p, q) for p in range(QUAD)] for q in range(BLOCKS)]
Q_GROUPS = [[seq_at(p, q) for q in range(BLOCKS)] for p in range(QUAD)]
ROW_GROUPS = [[seq_at(p, r * QUAD + c) for r in range(QUAD)] for p in range(QUAD) for c in range(QUAD)]
COLUMN_GROUPS = [[seq_at(p, r * QUAD + c) for c in range(QUAD)] for p in range(QUAD) for r in range(QUAD)]
NEG_FILL = -1e30
EPSILON = 1e-05
SCALE_LOG2 = math.log2(math.e) / math.sqrt(HD)
EXTRA = 16
PIECES = 4
MIB = 2**20


def dot_nt(a, b):
    return lax.dot_general(a, b, (((1,), (1,)), ((), ())), preferred_element_type=jnp.float32)


def parts_of(x, count):
    parts = []
    for _ in range(count):
        part = x.astype(jnp.bfloat16).astype(jnp.float32)
        parts.append(part)
        x = x - part
    return parts


def padded(rows, count):
    return jnp.concatenate(rows + [jnp.zeros_like(rows[0])] * (count - len(rows)), axis=0)


def with_ones(values):
    return jnp.concatenate([values.T, jnp.ones((EXTRA, values.shape[0]), values.dtype)], axis=0)


def bring(sources, targets, sems):
    waits = []
    for i, (source, target) in enumerate(zip(sources, targets)):
        size = source.shape[0] // PIECES
        copies = []
        for j in range(PIECES):
            part = pl.ds(j * size, size)
            copy = pltpu.make_async_copy(source.at[part], target.at[part], sems.at[i, j])
            copy.start()
            copies.append(copy)
        waits.append(lambda copies=copies: [copy.wait() for copy in copies])
    return waits


def own_place():
    seq = lax.axis_index("seq")
    return seq // SIDE % 2 * 2 + seq % 2


def head_rows(block, heads):
    return jnp.concatenate([block[:, h * HD : (h + 1) * HD] for h in range(heads)], axis=0)


def by_column(bands, band, numbers, shifts):
    size = numbers.shape[1]
    lane = lax.broadcasted_iota(jnp.int32, (bands, size), 1)
    mine = lane // band == lax.broadcasted_iota(jnp.int32, (bands, size), 0)
    digits = []
    for i, shift in enumerate(shifts):
        digit = lax.shift_right_logical(numbers, shift)
        if i > 0:
            digit = digit & 31
        digits.append(jnp.where(mine, digit.astype(jnp.float32), 0.0))
    row = lax.broadcasted_iota(jnp.int32, (size, size), 0)
    col = lax.broadcasted_iota(jnp.int32, (size, size), 1)
    spread = jnp.where(row % band == col % band, 1.0, 0.0).astype(jnp.bfloat16)
    got = jnp.dot(
        jnp.concatenate(digits, axis=0).astype(jnp.bfloat16), spread,
        preferred_element_type=jnp.float32,
    ).astype(jnp.int32)
    return sum(got[i * bands : (i + 1) * bands] << shift for i, shift in enumerate(shifts))


def attend(bands, band, heads, offsets_ref, lengths_ref, q_hbm, k_hbm, v_hbm, sk_hbm, sv_hbm, out_ref,
           q_ref, k_ref, v_ref, sk_ref, sv_ref, vt_ref, off_ref, len_ref, sems):
    context = k_ref.shape[0]
    tail = sk_ref.shape[1]
    cols = heads * band
    seq = lax.axis_index("seq")
    waits = bring(
        (q_hbm, k_hbm, sk_hbm, v_hbm, sv_hbm), (q_ref, k_ref, sk_ref, v_ref, sv_ref), sems
    )
    off_ref[...] = by_column(bands, band, offsets_ref[...], (10, 5, 0))
    len_ref[...] = by_column(bands, band, lengths_ref[...], (5, 0))

    def queries_of(g):
        return head_rows(q_ref[pl.ds(pl.multiple_of(g * band, band), band), :], heads)

    def pair(p, first):
        bases = (2 * p, 2 * p + 1)
        if first:
            waits[0]()
        qs = [queries_of(g) for g in bases]
        both = jnp.concatenate(qs, axis=0)
        offset = jnp.concatenate([off_ref[pl.ds(g, 1), :] for g in bases], axis=1)
        if first:
            waits[1]()
        scores = dot_nt(k_ref[...], both)
        pos = lax.broadcasted_iota(jnp.int32, scores.shape, 0)
        scores = jnp.where(pos < offset - seq * context, scores, NEG_FILL)
        peak = jnp.max(scores, axis=0, keepdims=True)
        tails = []
        if first:
            waits[2]()
        for i, g in enumerate(bases):
            at = pl.multiple_of(g * band, band)
            keys = sk_ref[pl.ds(at, band)].reshape(band * tail, HD)
            tail_scores = dot_nt(keys, qs[i])
            row = lax.broadcasted_iota(jnp.int32, tail_scores.shape, 0)
            col = lax.broadcasted_iota(jnp.int32, tail_scores.shape, 1)
            length = len_ref[pl.ds(g, 1), :] - seq * tail
            live = (row // tail == col % band) & (row % tail < length)
            tails.append(jnp.where(live, tail_scores, NEG_FILL))
        tail_peak = jnp.concatenate([jnp.max(t, axis=0, keepdims=True) for t in tails], axis=1)
        peak = jnp.maximum(peak, tail_peak)
        weights = jnp.exp2((scores - peak) * SCALE_LOG2).astype(jnp.bfloat16)
        if first:
            waits[3]()
            vt_ref[...] = with_ones(v_ref[...])
            waits[4]()
        sums = jnp.dot(vt_ref[...], weights, preferred_element_type=jnp.float32)
        for i, g in enumerate(bases):
            at = pl.multiple_of(g * band, band)
            own = slice(i * cols, (i + 1) * cols)
            own_peak = peak[:, own]
            tail_weights = jnp.exp2((tails[i] - own_peak) * SCALE_LOG2).astype(jnp.bfloat16)
            values = with_ones(sv_ref[pl.ds(at, band)].reshape(band * tail, HD))
            full = sums[:, own] + jnp.dot(values, tail_weights, preferred_element_type=jnp.float32)
            some = own_peak > 0.5 * NEG_FILL
            total = jnp.where(some, full[HD : HD + 1], 0.0)
            output = jnp.where(some, full[:HD], 0.0).T
            stats = padded(parts_of(own_peak, 3) + parts_of(total, 2), EXTRA)
            out_ref[g] = jnp.concatenate([output, stats], axis=0).astype(jnp.bfloat16)

    pair(0, True)
    pl.loop(1, bands // 2)(lambda p: pair(p, False))


def merged(got_ref):
    count, rows = got_ref.shape[0], got_ref.shape[1] - EXTRA
    stats = [got_ref[s, rows:].astype(jnp.float32) for s in range(count)]
    peaks = [st[0:1] + st[1:2] + st[2:3] for st in stats]
    totals = [st[3:4] + st[4:5] for st in stats]
    peak = functools.reduce(jnp.maximum, peaks)
    factors = [jnp.exp2((p - peak) * SCALE_LOG2) for p in peaks]
    total = sum(f * t for f, t in zip(factors, totals))
    columns = padded(factors + [peak, total], rows).T
    output = sum(
        columns[:, s : s + 1] * got_ref[s, :rows].astype(jnp.float32) for s in range(count)
    )
    return output, peak, total, columns[:, count : count + 1], columns[:, count + 1 : count + 2]


def merge(got_ref, out_ref):
    output, peak, total, _, _ = merged(got_ref)
    stats = padded(parts_of(peak, 3) + parts_of(total, 2), EXTRA)
    message = jnp.concatenate([output, stats], axis=0).astype(jnp.bfloat16)
    for i in range(out_ref.shape[0]):
        out_ref[i] = message


def finish(heads, band, got_ref, q_ref, nk_ref, nv_ref, out_ref):
    output, _, _, peak, total = merged(got_ref)
    own = pl.ds(pl.multiple_of(lax.axis_index("seq") // SIDE * band, band), band)
    tiled = lambda ref: jnp.concatenate([ref[own, :].astype(jnp.float32)] * heads, axis=0)
    query = head_rows(q_ref[own, :], heads).astype(jnp.float32)
    fresh = jnp.sum(query * tiled(nk_ref), axis=1, keepdims=True)
    row_peak = jnp.maximum(peak, fresh)
    factor = jnp.exp2((peak - row_peak) * SCALE_LOG2)
    fresh_factor = jnp.exp2((fresh - row_peak) * SCALE_LOG2)
    numerator = factor * output + fresh_factor * tiled(nv_ref)
    attention = (numerator / (factor * total + fresh_factor)).astype(jnp.bfloat16)
    for i in range(out_ref.shape[0]):
        out_ref[i] = attention


def arrange(gate_ref, up_ref, *outs):
    block = outs[0].shape[2]
    for k in range(QUAD):
        columns = pl.ds(pl.multiple_of((own_place() ^ k) * block, HD), block)
        outs[k][0] = gate_ref[:, columns]
        outs[k][1] = up_ref[:, columns]


def combine(got_ref, residual_ref, gain_ref, hidden_ref, out_ref):
    projected = sum(got_ref[k].astype(jnp.float32) for k in range(got_ref.shape[0]))
    hidden = (residual_ref[...].astype(jnp.float32) + projected).astype(jnp.bfloat16)
    hidden_ref[...] = hidden
    wide = hidden.astype(jnp.float32)
    squares = jnp.sum((wide * wide).T, axis=0, keepdims=True)
    message = jnp.concatenate(
        [wide * gain_ref[...], padded(parts_of(squares, 2), EXTRA)], axis=0
    ).astype(jnp.bfloat16)
    for p in range(QUAD):
        out_ref[p] = message


def gate_up(units, hidden_ref, *refs):
    weights, out_ref = refs[:QUAD], refs[QUAD]
    place = own_place()
    rows = hidden_ref.shape[1] - EXTRA
    totals = [None, None]
    squares = None
    for k in range(QUAD):
        message = hidden_ref[place ^ k]
        hidden = message[:rows]
        extra = message[rows:].astype(jnp.float32)
        row = extra[0:1] + extra[1:2]
        squares = row if squares is None else squares + row
        for i in range(2):
            term = jnp.dot(hidden, weights[k][i], preferred_element_type=jnp.float32)
            totals[i] = term if totals[i] is None else totals[i] + term
    gate, up = [total.T for total in totals]
    extra = padded(parts_of(squares, 2), EXTRA)
    for q in range(BLOCKS):
        part = slice(units * q, units * (q + 1))
        out_ref[q] = jnp.concatenate([gate[part], up[part], extra], axis=0).astype(jnp.bfloat16)


def activate(units, pad, got_ref, out_ref):
    sums = sum(got_ref[q].astype(jnp.float32) for q in range(BLOCKS))
    mean_square = (sums[2 * units : 2 * units + 1] + sums[2 * units + 1 : 2 * units + 2]) / D
    inverse = lax.rsqrt(mean_square + EPSILON)
    gate, up = sums[:units] * inverse, sums[units : 2 * units] * inverse
    activation = gate / (1.0 + jnp.exp(-gate)) * up
    zeros = jnp.zeros((pad - units, activation.shape[1]), jnp.float32)
    message = jnp.concatenate([activation, zeros], axis=0).astype(jnp.bfloat16)
    for i in range(out_ref.shape[0]):
        out_ref[i] = message


def down(units, act_ref, *refs):
    weights, out_ref = refs[:QUAD], refs[QUAD]
    place = own_place()
    rows = [
        act_ref[q % QUAD, q // QUAD].astype(jnp.float32)[:units] for q in range(BLOCKS)
    ]
    act = jnp.concatenate(rows, axis=0).T.astype(jnp.bfloat16)
    for k in range(QUAD):
        term = jnp.dot(act, weights[k][...], preferred_element_type=jnp.float32)
        out_ref[place ^ k] = term.astype(jnp.bfloat16)


def call(kernel, outs, name, *args, hbm=(), scratch=()):
    spec = lambda i: pl.BlockSpec(memory_space=pl.ANY if i in hbm else pltpu.VMEM)
    return pl.pallas_call(
        kernel,
        out_shape=outs,
        in_specs=[spec(i) for i in range(len(args))],
        scratch_shapes=scratch,
        compiler_params=pltpu.CompilerParams(vmem_limit_bytes=(56 if hbm else 32) * MIB),
        name=name,
    )(*args)


def exchange(x, groups):
    return lax.all_to_all(x, "seq", 0, 0, axis_index_groups=groups, tiled=True)


def gather(x, axis, count, groups=None):
    copies = jnp.broadcast_to(x, (count,) + x.shape)
    return lax.all_to_all(copies, axis, 0, 0, axis_index_groups=groups, tiled=True)


def on_device(n_kvh, queries, new_keys, new_values, prefix_keys, prefix_values, suffix_keys,
              suffix_values, prefix_offsets, suffix_lengths, out_weight, residual, norm_gain,
              w_gate, w_up, w_down):
    branches, width = residual.shape
    heads = queries.shape[1] // HD
    bands = SIDE
    band = branches // bands
    rows = heads * band
    hidden_units = w_gate.shape[1]
    units = hidden_units // SIDE**2
    pad = -(-units // 16) * 16
    bf16 = lambda *shape: jax.ShapeDtypeStruct(shape, jnp.bfloat16)
    like = lambda a: pltpu.VMEM(a.shape, a.dtype)
    copies_sem = lambda n: pltpu.SemaphoreType.DMA((n, PIECES))

    message = call(
        functools.partial(attend, bands, band, heads),
        bf16(bands, rows + EXTRA, HD),
        "attend",
        prefix_offsets.reshape(1, branches), suffix_lengths.reshape(1, branches), queries,
        prefix_keys, prefix_values, suffix_keys, suffix_values,
        hbm=(2, 3, 4, 5, 6),
        scratch=[like(queries), like(prefix_keys), like(prefix_values), like(suffix_keys),
                 like(suffix_values),
                 pltpu.VMEM((HD + EXTRA, prefix_keys.shape[0]), jnp.bfloat16),
                 pltpu.VMEM((bands, rows), jnp.int32), pltpu.VMEM((bands, rows), jnp.int32),
                 copies_sem(5)],
    )
    message, *moved = lax.optimization_barrier((message, w_gate, w_up))
    block = hidden_units // QUAD
    mine = call(arrange, (bf16(2, width, block),) * QUAD, "arrange", *moved)
    swap = lambda x, k: lax.ppermute(
        x, "seq", [(seq_at(p, q), seq_at(p ^ k, q)) for q in range(BLOCKS) for p in range(QUAD)]
    )
    def step(value, arrived, operand, k):
        value, arrived, operand = lax.optimization_barrier((value, arrived, operand))
        return value, arrived, swap(operand, k)

    both = [mine[0], swap(mine[1], 1)]
    message = call(merge, bf16(SIDE, rows + EXTRA, HD), "merge", exchange(message, Z_GROUPS))
    message, both[1], coming = step(message, both[1], mine[2], 2)
    own = call(
        functools.partial(finish, heads, band), bf16(SIDE, rows, HD), "finish",
        exchange(message, Y_GROUPS), queries, new_keys, new_values,
    )
    own, coming, last = step(own, coming, mine[3], 3)
    both.append(coming)
    gathered = exchange(own, Z_GROUPS)
    pieces = [
        lax.dynamic_slice_in_dim(w_down, (own_place() ^ k) * block, block) for k in range(QUAD)
    ]
    gathered, last, coming = step(gathered, last, pieces[1], 1)
    both.append(last)
    downs = [pieces[0]]
    attention = (
        gathered.reshape(bands, heads, band, HD).transpose(0, 2, 1, 3).reshape(branches, heads * HD)
    )

    projected = jnp.dot(attention, out_weight, preferred_element_type=jnp.float32)
    hidden, message = call(
        combine, (bf16(branches, width), bf16(QUAD, branches + EXTRA, width)), "combine",
        gather(projected.astype(jnp.bfloat16), "kvh", n_kvh), residual, norm_gain.reshape(1, width),
    )
    message, coming, following = step(message, coming, pieces[2], 2)
    downs.append(coming)
    hiddens, following, last = step(exchange(message, P_GROUPS), following, pieces[3], 3)
    downs.append(following)
    message = call(
        functools.partial(gate_up, units), bf16(BLOCKS, 2 * units + EXTRA, branches), "gate_up",
        hiddens, *both,
    )
    message = call(
        functools.partial(activate, units, pad), bf16(QUAD, pad, branches), "activate",
        exchange(message, Q_GROUPS),
    )
    message, last = lax.optimization_barrier((message, last))
    downs.append(last)
    rows_of_blocks = exchange(message, ROW_GROUPS)
    message = call(
        functools.partial(down, units), bf16(QUAD, branches, width), "down",
        gather(rows_of_blocks, "seq", QUAD, COLUMN_GROUPS), *downs,
    )
    ffn_part = jnp.sum(exchange(message, P_GROUPS).astype(jnp.float32), axis=0)
    terms = gather(ffn_part.astype(jnp.bfloat16), "kvh", n_kvh)
    ffn_sum = jnp.sum(terms.astype(jnp.float32), axis=0)
    mixed = (hidden.astype(jnp.float32) + ffn_sum).astype(jnp.bfloat16)
    return (attention, mixed)


def solution(mesh):
    return jax.shard_map(
        functools.partial(on_device, mesh.shape["kvh"]),
        mesh=mesh,
        in_specs=(
            P(None, "kvh"),
            P(None, "kvh"),
            P(None, "kvh"),
            P("seq", "kvh"),
            P("seq", "kvh"),
            P(None, "seq", "kvh"),
            P(None, "seq", "kvh"),
            P(),
            P(),
            P("kvh", "seq"),
            P(None, "seq"),
            P("seq"),
            P("seq", "kvh"),
            P("seq", "kvh"),
            P("kvh", "seq"),
        ),
        out_specs=(P(None, "kvh"), P(None, "seq")),
        check_vma=False,
    )
```

```python
import functools
import math

import jax
import jax.numpy as jnp
from jax import lax
from jax.experimental import pallas as pl
from jax.experimental.pallas import tpu as pltpu
from jax.sharding import PartitionSpec as P

HD = 128
D = 8192
SIDE = 8
Z_GROUPS = [[z * SIDE + y for z in range(SIDE)] for y in range(SIDE)]
Y_GROUPS = [[z * SIDE + y for y in range(SIDE)] for z in range(SIDE)]
QUAD = 4
BLOCKS = SIDE * SIDE // QUAD


def seq_at(p, q):
    return (q // (SIDE // 2) * 2 + p // 2) * SIDE + q % (SIDE // 2) * 2 + p % 2


P_GROUPS = [[seq_at(p, q) for p in range(QUAD)] for q in range(BLOCKS)]
Q_GROUPS = [[seq_at(p, q) for q in range(BLOCKS)] for p in range(QUAD)]
SEQ_ORDER = [seq_at(p, q) for p in range(QUAD) for q in range(BLOCKS)]
NEG_FILL = -1e30
EPSILON = 1e-05
SCALE_LOG2 = math.log2(math.e) / math.sqrt(HD)
EXTRA = 16
PIECES = 4
MIB = 2**20


def dot_nt(a, b):
    return lax.dot_general(a, b, (((1,), (1,)), ((), ())), preferred_element_type=jnp.float32)


def parts_of(x, count):
    parts = []
    for _ in range(count):
        part = x.astype(jnp.bfloat16).astype(jnp.float32)
        parts.append(part)
        x = x - part
    return parts


def padded(rows, count):
    return jnp.concatenate(rows + [jnp.zeros_like(rows[0])] * (count - len(rows)), axis=0)


def with_ones(values):
    return jnp.concatenate([values.T, jnp.ones((EXTRA, values.shape[0]), values.dtype)], axis=0)


def bring(sources, targets, sems):
    waits = []
    for i, (source, target) in enumerate(zip(sources, targets)):
        size = source.shape[0] // PIECES
        copies = []
        for j in range(PIECES):
            part = pl.ds(j * size, size)
            copy = pltpu.make_async_copy(source.at[part], target.at[part], sems.at[i, j])
            copy.start()
            copies.append(copy)
        waits.append(lambda copies=copies: [copy.wait() for copy in copies])
    return waits


def own_place():
    seq = lax.axis_index("seq")
    return seq // SIDE % 2 * 2 + seq % 2


def head_rows(block, heads):
    return jnp.concatenate([block[:, h * HD : (h + 1) * HD] for h in range(heads)], axis=0)


def over(x, power):
    assert power & (power - 1) == 0
    return lax.shift_right_logical(x, power.bit_length() - 1)


def by_column(bands, band, numbers, shifts):
    size = numbers.shape[1]
    lane = lax.broadcasted_iota(jnp.int32, (bands, size), 1)
    mine = over(lane, band) == lax.broadcasted_iota(jnp.int32, (bands, size), 0)
    digits = []
    for i, shift in enumerate(shifts):
        digit = lax.shift_right_logical(numbers, shift)
        if i > 0:
            digit = digit & 31
        digits.append(jnp.where(mine, digit.astype(jnp.float32), 0.0))
    row = lax.broadcasted_iota(jnp.int32, (size, size), 0)
    col = lax.broadcasted_iota(jnp.int32, (size, size), 1)
    spread = jnp.where(row & (band - 1) == col & (band - 1), 1.0, 0.0).astype(jnp.bfloat16)
    got = jnp.dot(
        jnp.concatenate(digits, axis=0).astype(jnp.bfloat16), spread,
        preferred_element_type=jnp.float32,
    ).astype(jnp.int32)
    return sum(got[i * bands : (i + 1) * bands] << shift for i, shift in enumerate(shifts))


def attend(bands, band, heads, offsets_ref, lengths_ref, q_hbm, k_hbm, v_hbm, sk_hbm, sv_hbm, out_ref,
           q_ref, k_ref, v_ref, sk_ref, sv_ref, vt_ref, off_ref, len_ref, tail_pos_ref,
           sems):
    context = k_ref.shape[0]
    tail = sk_ref.shape[1]
    cols = heads * band
    seq = lax.axis_index("seq")
    waits = bring(
        (q_hbm, k_hbm, sk_hbm, v_hbm, sv_hbm), (q_ref, k_ref, sk_ref, v_ref, sv_ref), sems
    )
    off_ref[...] = by_column(bands, band, offsets_ref[...], (10, 5, 0))
    len_ref[...] = by_column(bands, band, lengths_ref[...], (5, 0))
    row = lax.broadcasted_iota(jnp.int32, tail_pos_ref.shape, 0)
    col = lax.broadcasted_iota(jnp.int32, tail_pos_ref.shape, 1)
    own_branch = over(row, tail) == col & (band - 1)
    tail_pos_ref[...] = jnp.where(own_branch, row & (tail - 1), 2**20)

    def queries_of(g):
        return head_rows(q_ref[pl.ds(pl.multiple_of(g * band, band), band), :], heads)

    def pair(p, first):
        bases = (2 * p, 2 * p + 1)
        if first:
            waits[0]()
        qs = [queries_of(g) for g in bases]
        both = jnp.concatenate(qs, axis=0)
        offset = jnp.concatenate([off_ref[pl.ds(g, 1), :] for g in bases], axis=1)
        if first:
            waits[1]()
        scores = dot_nt(k_ref[...], both)
        pos = lax.broadcasted_iota(jnp.int32, scores.shape, 0)
        scores = jnp.where(pos < offset - seq * context, scores, NEG_FILL)
        peak = jnp.max(scores, axis=0, keepdims=True)
        tails = []
        if first:
            waits[2]()
        for i, g in enumerate(bases):
            at = pl.multiple_of(g * band, band)
            keys = sk_ref[pl.ds(at, band)].reshape(band * tail, HD)
            tail_scores = dot_nt(keys, qs[i])
            length = len_ref[pl.ds(g, 1), :] - seq * tail
            tails.append(jnp.where(tail_pos_ref[...] < length, tail_scores, NEG_FILL))
        tail_peak = jnp.concatenate([jnp.max(t, axis=0, keepdims=True) for t in tails], axis=1)
        peak = jnp.maximum(peak, tail_peak)
        weights = jnp.exp2((scores - peak) * SCALE_LOG2).astype(jnp.bfloat16)
        if first:
            waits[3]()
            vt_ref[...] = with_ones(v_ref[...])
            waits[4]()
        sums = jnp.dot(vt_ref[...], weights, preferred_element_type=jnp.float32)
        for i, g in enumerate(bases):
            at = pl.multiple_of(g * band, band)
            own = slice(i * cols, (i + 1) * cols)
            own_peak = peak[:, own]
            tail_weights = jnp.exp2((tails[i] - own_peak) * SCALE_LOG2).astype(jnp.bfloat16)
            values = with_ones(sv_ref[pl.ds(at, band)].reshape(band * tail, HD))
            full = sums[:, own] + jnp.dot(values, tail_weights, preferred_element_type=jnp.float32)
            some = own_peak > 0.5 * NEG_FILL
            total = jnp.where(some, full[HD : HD + 1], 0.0)
            output = jnp.where(some, full[:HD], 0.0).T
            stats = padded(parts_of(own_peak, 3) + parts_of(total, 2), EXTRA)
            out_ref[g] = jnp.concatenate([output, stats], axis=0).astype(jnp.bfloat16)

    pair(0, True)
    pl.loop(1, bands // 2)(lambda p: pair(p, False))


def merged(got_ref):
    count, rows = got_ref.shape[0], got_ref.shape[1] - EXTRA
    stats = [got_ref[s, rows:].astype(jnp.float32) for s in range(count)]
    peaks = [st[0:1] + st[1:2] + st[2:3] for st in stats]
    totals = [st[3:4] + st[4:5] for st in stats]
    peak = functools.reduce(jnp.maximum, peaks)
    factors = [jnp.exp2((p - peak) * SCALE_LOG2) for p in peaks]
    total = sum(f * t for f, t in zip(factors, totals))
    columns = padded(factors + [peak, total], rows).T
    output = sum(
        columns[:, s : s + 1] * got_ref[s, :rows].astype(jnp.float32) for s in range(count)
    )
    return output, peak, total, columns[:, count : count + 1], columns[:, count + 1 : count + 2]


def merge(got_ref, out_ref):
    output, peak, total, _, _ = merged(got_ref)
    stats = padded(parts_of(peak, 3) + parts_of(total, 2), EXTRA)
    message = jnp.concatenate([output, stats], axis=0).astype(jnp.bfloat16)
    for i in range(out_ref.shape[0]):
        out_ref[i] = message


def finish(heads, band, got_ref, q_ref, nk_ref, nv_ref, out_ref):
    output, _, _, peak, total = merged(got_ref)
    own = pl.ds(pl.multiple_of(lax.axis_index("seq") // SIDE * band, band), band)
    tiled = lambda ref: jnp.concatenate([ref[own, :].astype(jnp.float32)] * heads, axis=0)
    query = head_rows(q_ref[own, :], heads).astype(jnp.float32)
    fresh = jnp.sum(query * tiled(nk_ref), axis=1, keepdims=True)
    row_peak = jnp.maximum(peak, fresh)
    factor = jnp.exp2((peak - row_peak) * SCALE_LOG2)
    fresh_factor = jnp.exp2((fresh - row_peak) * SCALE_LOG2)
    numerator = factor * output + fresh_factor * tiled(nv_ref)
    attention = (numerator / (factor * total + fresh_factor)).astype(jnp.bfloat16)
    for i in range(out_ref.shape[0]):
        out_ref[i] = attention


def arrange(gate_ref, up_ref, *outs):
    block = outs[0].shape[2]
    for k in range(QUAD):
        columns = pl.ds(pl.multiple_of((own_place() ^ k) * block, HD), block)
        outs[k][0] = gate_ref[:, columns]
        outs[k][1] = up_ref[:, columns]


def combine(got_ref, residual_ref, gain_ref, hidden_ref, out_ref):
    projected = sum(got_ref[k].astype(jnp.float32) for k in range(got_ref.shape[0]))
    hidden = (residual_ref[...].astype(jnp.float32) + projected).astype(jnp.bfloat16)
    hidden_ref[...] = hidden
    wide = hidden.astype(jnp.float32)
    squares = jnp.sum((wide * wide).T, axis=0, keepdims=True)
    message = jnp.concatenate(
        [wide * gain_ref[...], padded(parts_of(squares, 2), EXTRA)], axis=0
    ).astype(jnp.bfloat16)
    for p in range(QUAD):
        out_ref[p] = message


def gate_up(units, hidden_ref, *refs):
    weights, out_ref = refs[:QUAD], refs[QUAD]
    place = own_place()
    rows = hidden_ref.shape[1] - EXTRA
    totals = [None, None]
    squares = None
    for k in range(QUAD):
        message = hidden_ref[place ^ k]
        hidden = message[:rows]
        extra = message[rows:].astype(jnp.float32)
        row = extra[0:1] + extra[1:2]
        squares = row if squares is None else squares + row
        for i in range(2):
            term = jnp.dot(hidden, weights[k][i], preferred_element_type=jnp.float32)
            totals[i] = term if totals[i] is None else totals[i] + term
    gate, up = [total.T for total in totals]
    extra = padded(parts_of(squares, 2), EXTRA)
    for q in range(BLOCKS):
        part = slice(units * q, units * (q + 1))
        out_ref[q] = jnp.concatenate([gate[part], up[part], extra], axis=0).astype(jnp.bfloat16)


def activate(units, got_ref, out_ref):
    sums = sum(got_ref[q].astype(jnp.float32) for q in range(BLOCKS))
    mean_square = (sums[2 * units : 2 * units + 1] + sums[2 * units + 1 : 2 * units + 2]) / D
    inverse = lax.rsqrt(mean_square + EPSILON)
    gate, up = sums[:units] * inverse, sums[units : 2 * units] * inverse
    activation = gate / (1.0 + jnp.exp(-gate)) * up
    zeros = jnp.zeros((out_ref.shape[0] - units, activation.shape[1]), jnp.float32)
    out_ref[...] = jnp.concatenate([activation, zeros], axis=0).astype(jnp.bfloat16)


def call(kernel, outs, name, *args, hbm=(), scratch=()):
    spec = lambda i: pl.BlockSpec(memory_space=pl.ANY if i in hbm else pltpu.VMEM)
    return pl.pallas_call(
        kernel,
        out_shape=outs,
        in_specs=[spec(i) for i in range(len(args))],
        scratch_shapes=scratch,
        compiler_params=pltpu.CompilerParams(vmem_limit_bytes=(56 if hbm else 32) * MIB),
        name=name,
    )(*args)


def exchange(x, groups):
    return lax.all_to_all(x, "seq", 0, 0, axis_index_groups=groups, tiled=True)


def gather(x, axis, count, groups=None):
    copies = jnp.broadcast_to(x, (count,) + x.shape)
    return lax.all_to_all(copies, axis, 0, 0, axis_index_groups=groups, tiled=True)


def on_device(n_kvh, queries, new_keys, new_values, prefix_keys, prefix_values, suffix_keys,
              suffix_values, prefix_offsets, suffix_lengths, out_weight, residual, norm_gain,
              w_gate, w_up, w_down):
    branches, width = residual.shape
    heads = queries.shape[1] // HD
    bands = SIDE
    band = branches // bands
    rows = heads * band
    hidden_units = w_gate.shape[1]
    units = hidden_units // SIDE**2
    pad = -(-units // 16) * 16
    bf16 = lambda *shape: jax.ShapeDtypeStruct(shape, jnp.bfloat16)
    like = lambda a: pltpu.VMEM(a.shape, a.dtype)
    copies_sem = lambda n: pltpu.SemaphoreType.DMA((n, PIECES))

    message = call(
        functools.partial(attend, bands, band, heads),
        bf16(bands, rows + EXTRA, HD),
        "attend",
        prefix_offsets.reshape(1, branches), suffix_lengths.reshape(1, branches), queries,
        prefix_keys, prefix_values, suffix_keys, suffix_values,
        hbm=(2, 3, 4, 5, 6),
        scratch=[like(queries), like(prefix_keys), like(prefix_values), like(suffix_keys),
                 like(suffix_values),
                 pltpu.VMEM((HD + EXTRA, prefix_keys.shape[0]), jnp.bfloat16),
                 pltpu.VMEM((bands, rows), jnp.int32), pltpu.VMEM((bands, rows), jnp.int32),
                 pltpu.VMEM((band * suffix_keys.shape[1], rows), jnp.int32),
                 copies_sem(5)],
    )
    message, *moved = lax.optimization_barrier((message, w_gate, w_up))
    block = hidden_units // QUAD
    mine = call(arrange, (bf16(2, width, block),) * QUAD, "arrange", *moved)
    swap = lambda x, k: lax.ppermute(
        x, "seq", [(seq_at(p, q), seq_at(p ^ k, q)) for q in range(BLOCKS) for p in range(QUAD)]
    )
    both = [mine[0]] + [swap(mine[k], k) for k in range(1, QUAD)]

    message = call(merge, bf16(SIDE, rows + EXTRA, HD), "merge", exchange(message, Z_GROUPS))
    own = call(
        functools.partial(finish, heads, band), bf16(SIDE, rows, HD), "finish",
        exchange(message, Y_GROUPS), queries, new_keys, new_values,
    )
    gathered = exchange(own, Z_GROUPS)
    attention = (
        gathered.reshape(bands, heads, band, HD).transpose(0, 2, 1, 3).reshape(branches, heads * HD)
    )

    projected = jnp.dot(attention, out_weight, preferred_element_type=jnp.float32)
    hidden, message = call(
        combine, (bf16(branches, width), bf16(QUAD, branches + EXTRA, width)), "combine",
        gather(projected.astype(jnp.bfloat16), "kvh", n_kvh), residual, norm_gain.reshape(1, width),
    )
    message, *both = lax.optimization_barrier((message, *both))
    message = call(
        functools.partial(gate_up, units), bf16(BLOCKS, 2 * units + EXTRA, branches), "gate_up",
        exchange(message, P_GROUPS), *both,
    )
    activation = call(
        functools.partial(activate, units), bf16(pad, branches), "activate",
        exchange(message, Q_GROUPS),
    )[:units]
    activations = gather(activation, "seq", SIDE * SIDE, [SEQ_ORDER]).reshape(hidden_units, branches)
    ffn_part = lax.dot_general(
        activations, w_down, (((0,), (0,)), ((), ())), preferred_element_type=jnp.float32
    )
    terms = gather(ffn_part.astype(jnp.bfloat16), "kvh", n_kvh)
    ffn_sum = jnp.sum(terms.astype(jnp.float32), axis=0)
    mixed = (hidden.astype(jnp.float32) + ffn_sum).astype(jnp.bfloat16)
    return (attention, mixed)


def solution(mesh):
    return jax.shard_map(
        functools.partial(on_device, mesh.shape["kvh"]),
        mesh=mesh,
        in_specs=(
            P(None, "kvh"),
            P(None, "kvh"),
            P(None, "kvh"),
            P("seq", "kvh"),
            P("seq", "kvh"),
            P(None, "seq", "kvh"),
            P(None, "seq", "kvh"),
            P(),
            P(),
            P("kvh", "seq"),
            P(None, "seq"),
            P("seq"),
            P("seq", "kvh"),
            P("seq", "kvh"),
            P("kvh", "seq"),
        ),
        out_specs=(P(None, "kvh"), P(None, "seq")),
        check_vma=False,
    )
```

```python
import functools
import math

import jax
import jax.numpy as jnp
from jax import lax
from jax.experimental import pallas as pl
from jax.experimental.pallas import tpu as pltpu
from jax.sharding import PartitionSpec as P

HD = 128
D = 8192
SIDE = 8
QUAD = 4
BLOCKS = SIDE * SIDE // QUAD


def seq_at(p, q):
    return (q // (SIDE // 2) * 2 + p // 2) * SIDE + q % (SIDE // 2) * 2 + p % 2


P_GROUPS = [[seq_at(p, q) for p in range(QUAD)] for q in range(BLOCKS)]
Q_GROUPS = [[seq_at(p, q) for q in range(BLOCKS)] for p in range(QUAD)]
SEQ_ORDER = [seq_at(p, q) for p in range(QUAD) for q in range(BLOCKS)]
NEG_FILL = -1e30
EPSILON = 1e-05
SCALE_LOG2 = math.log2(math.e) / math.sqrt(HD)
STATS = 8
EXTRA = 16
PIECES = 4
MIB = 2**20


def dot_nt(a, b):
    return lax.dot_general(a, b, (((1,), (1,)), ((), ())), preferred_element_type=jnp.float32)


def parts_of(x, count):
    parts = []
    for _ in range(count):
        part = x.astype(jnp.bfloat16).astype(jnp.float32)
        parts.append(part)
        x = x - part
    return parts


def padded(rows, count):
    return jnp.concatenate(rows + [jnp.zeros_like(rows[0])] * (count - len(rows)), axis=0)


def with_ones(values):
    return jnp.concatenate([values.T, jnp.ones((EXTRA, values.shape[0]), values.dtype)], axis=0)


def bring(sources, targets, sems):
    waits = []
    for i, (source, target) in enumerate(zip(sources, targets)):
        size = source.shape[0] // PIECES
        copies = []
        for j in range(PIECES):
            part = pl.ds(j * size, size)
            copy = pltpu.make_async_copy(source.at[part], target.at[part], sems.at[i, j])
            copy.start()
            copies.append(copy)
        waits.append(lambda copies=copies: [copy.wait() for copy in copies])
    return waits


def own_place():
    seq = lax.axis_index("seq")
    return seq // SIDE % 2 * 2 + seq % 2


def head_rows(block, heads):
    return jnp.concatenate([block[:, h * HD : (h + 1) * HD] for h in range(heads)], axis=0)


def over(x, power):
    assert power & (power - 1) == 0
    return lax.shift_right_logical(x, power.bit_length() - 1)


def by_column(bands, band, numbers, shifts):
    size = numbers.shape[1]
    lane = lax.broadcasted_iota(jnp.int32, (bands, size), 1)
    mine = over(lane, band) == lax.broadcasted_iota(jnp.int32, (bands, size), 0)
    digits = []
    for i, shift in enumerate(shifts):
        digit = lax.shift_right_logical(numbers, shift)
        if i > 0:
            digit = digit & 31
        digits.append(jnp.where(mine, digit.astype(jnp.float32), 0.0))
    row = lax.broadcasted_iota(jnp.int32, (size, size), 0)
    col = lax.broadcasted_iota(jnp.int32, (size, size), 1)
    spread = jnp.where(row & (band - 1) == col & (band - 1), 1.0, 0.0).astype(jnp.bfloat16)
    got = jnp.dot(
        jnp.concatenate(digits, axis=0).astype(jnp.bfloat16), spread,
        preferred_element_type=jnp.float32,
    ).astype(jnp.int32)
    return sum(got[i * bands : (i + 1) * bands] << shift for i, shift in enumerate(shifts))


def attend(bands, band, heads, offsets_ref, lengths_ref, q_hbm, k_hbm, v_hbm, sk_hbm, sv_hbm, out_ref,
           q_ref, k_ref, v_ref, sk_ref, sv_ref, vt_ref, off_ref, len_ref, tail_pos_ref,
           weight_ref, tail_weight_ref, peak_ref, sems):
    context = k_ref.shape[0]
    tail = sk_ref.shape[1]
    cols = heads * band
    seq = lax.axis_index("seq")
    waits = bring(
        (q_hbm, k_hbm, sk_hbm, v_hbm, sv_hbm), (q_ref, k_ref, sk_ref, v_ref, sv_ref), sems
    )
    off_ref[...] = by_column(bands, band, offsets_ref[...], (10, 5, 0))
    len_ref[...] = by_column(bands, band, lengths_ref[...], (5, 0))
    row = lax.broadcasted_iota(jnp.int32, tail_pos_ref.shape, 0)
    col = lax.broadcasted_iota(jnp.int32, tail_pos_ref.shape, 1)
    own_branch = over(row, tail) == col & (band - 1)
    tail_pos_ref[...] = jnp.where(own_branch, row & (tail - 1), 2**20)

    def queries_of(g):
        return head_rows(q_ref[pl.ds(pl.multiple_of(g * band, band), band), :], heads)

    def weigh(p, first):
        bases = (2 * p, 2 * p + 1)
        if first:
            waits[0]()
        qs = [queries_of(g) for g in bases]
        both = jnp.concatenate(qs, axis=0)
        offset = jnp.concatenate([off_ref[pl.ds(g, 1), :] for g in bases], axis=1)
        if first:
            waits[1]()
        scores = dot_nt(k_ref[...], both)
        pos = lax.broadcasted_iota(jnp.int32, scores.shape, 0)
        scores = jnp.where(pos < offset - seq * context, scores, NEG_FILL)
        peak = jnp.max(scores, axis=0, keepdims=True)
        tails = []
        if first:
            waits[2]()
        for i, g in enumerate(bases):
            at = pl.multiple_of(g * band, band)
            keys = sk_ref[pl.ds(at, band)].reshape(band * tail, HD)
            tail_scores = dot_nt(keys, qs[i])
            length = len_ref[pl.ds(g, 1), :] - seq * tail
            tails.append(jnp.where(tail_pos_ref[...] < length, tail_scores, NEG_FILL))
        tail_peak = jnp.concatenate([jnp.max(t, axis=0, keepdims=True) for t in tails], axis=1)
        peak = jnp.maximum(peak, tail_peak)
        weight_ref[p] = jnp.exp2((scores - peak) * SCALE_LOG2).astype(jnp.bfloat16)
        for i, g in enumerate(bases):
            own_peak = peak[:, i * cols : (i + 1) * cols]
            peak_ref[pl.ds(g, 1), :] = own_peak
            tail_weight_ref[g] = jnp.exp2((tails[i] - own_peak) * SCALE_LOG2).astype(jnp.bfloat16)

    def add_up(p):
        sums = jnp.dot(vt_ref[...], weight_ref[p], preferred_element_type=jnp.float32)
        for i, g in enumerate((2 * p, 2 * p + 1)):
            at = pl.multiple_of(g * band, band)
            values = with_ones(sv_ref[pl.ds(at, band)].reshape(band * tail, HD))
            full = sums[:, i * cols : (i + 1) * cols] + jnp.dot(
                values, tail_weight_ref[g], preferred_element_type=jnp.float32
            )
            own_peak = peak_ref[pl.ds(g, 1), :]
            some = own_peak > 0.5 * NEG_FILL
            total = jnp.where(some, full[HD : HD + 1], 0.0)
            output = jnp.where(some, full[:HD], 0.0).T
            stats = padded(parts_of(own_peak, 3) + parts_of(total, 2), STATS)
            for h in range(heads):
                message = jnp.concatenate([output[h * band : (h + 1) * band], stats], axis=0)
                out_ref[g * heads + h] = message.astype(jnp.bfloat16)

    weigh(0, True)
    pl.loop(1, bands // 2)(lambda p: weigh(p, False))
    waits[3]()
    vt_ref[...] = with_ones(v_ref[...])
    waits[4]()
    pl.loop(0, bands // 2)(add_up)


def finish(heads, band, got_ref, q_ref, nk_ref, nv_ref, out_ref, columns_ref):
    count = got_ref.shape[0]
    seq = lax.axis_index("seq")
    own_band, own_head = seq // heads, seq % heads
    got = got_ref[...].astype(jnp.float32)
    stats = got[:, band:]
    kind = lax.broadcasted_iota(jnp.int32, stats.shape, 1)
    peaks = jnp.sum(jnp.where(kind < 3, stats, 0.0), axis=1)
    totals = jnp.sum(jnp.where(kind >= 3, stats, 0.0), axis=1)
    peak = jnp.max(peaks, axis=0, keepdims=True)
    factors = jnp.exp2((peaks - peak) * SCALE_LOG2)
    total = jnp.sum(factors * totals, axis=0, keepdims=True)
    zeros = jnp.zeros((peaks.shape[1] - count - 2, peaks.shape[1]), jnp.float32)
    columns_ref[...] = jnp.concatenate([factors, peak, total, zeros], axis=0).T
    columns = columns_ref[pl.ds(pl.multiple_of(own_head * band, band), band), :]
    output = sum(columns[:, s : s + 1] * got[s, :band] for s in range(count))
    peak, total = columns[:, count : count + 1], columns[:, count + 1 : count + 2]
    own = pl.ds(pl.multiple_of(own_band * band, band), band)
    query = q_ref[own, pl.ds(pl.multiple_of(own_head * HD, HD), HD)].astype(jnp.float32)
    fresh = jnp.sum(query * nk_ref[own, :].astype(jnp.float32), axis=1, keepdims=True)
    row_peak = jnp.maximum(peak, fresh)
    factor = jnp.exp2((peak - row_peak) * SCALE_LOG2)
    fresh_factor = jnp.exp2((fresh - row_peak) * SCALE_LOG2)
    numerator = factor * output + fresh_factor * nv_ref[own, :].astype(jnp.float32)
    attention = (numerator / (factor * total + fresh_factor)).astype(jnp.bfloat16)
    for i in range(out_ref.shape[0]):
        out_ref[i] = attention


def arrange(gate_ref, up_ref, *outs):
    block = outs[0].shape[2]
    for k in range(QUAD):
        columns = pl.ds(pl.multiple_of((own_place() ^ k) * block, HD), block)
        outs[k][0] = gate_ref[:, columns]
        outs[k][1] = up_ref[:, columns]


def combine(got_ref, residual_ref, gain_ref, hidden_ref, out_ref):
    projected = sum(got_ref[k].astype(jnp.float32) for k in range(got_ref.shape[0]))
    hidden = (residual_ref[...].astype(jnp.float32) + projected).astype(jnp.bfloat16)
    hidden_ref[...] = hidden
    wide = hidden.astype(jnp.float32)
    squares = jnp.sum((wide * wide).T, axis=0, keepdims=True)
    message = jnp.concatenate(
        [wide * gain_ref[...], padded(parts_of(squares, 2), EXTRA)], axis=0
    ).astype(jnp.bfloat16)
    for p in range(QUAD):
        out_ref[p] = message


def gate_up(units, hidden_ref, *refs):
    weights, out_ref = refs[:QUAD], refs[QUAD]
    place = own_place()
    rows = hidden_ref.shape[1] - EXTRA
    totals = [None, None]
    squares = None
    for k in range(QUAD):
        message = hidden_ref[place ^ k]
        hidden = message[:rows]
        extra = message[rows:].astype(jnp.float32)
        row = extra[0:1] + extra[1:2]
        squares = row if squares is None else squares + row
        for i in range(2):
            term = jnp.dot(hidden, weights[k][i], preferred_element_type=jnp.float32)
            totals[i] = term if totals[i] is None else totals[i] + term
    gate, up = [total.T for total in totals]
    extra = padded(parts_of(squares, 2), STATS)
    for q in range(BLOCKS):
        part = slice(units * q, units * (q + 1))
        out_ref[q] = jnp.concatenate([gate[part], up[part], extra], axis=0).astype(jnp.bfloat16)


def activate(units, got_ref, out_ref):
    sums = sum(got_ref[q].astype(jnp.float32) for q in range(BLOCKS))
    mean_square = (sums[2 * units : 2 * units + 1] + sums[2 * units + 1 : 2 * units + 2]) / D
    inverse = lax.rsqrt(mean_square + EPSILON)
    gate, up = sums[:units] * inverse, sums[units : 2 * units] * inverse
    activation = gate / (1.0 + jnp.exp(-gate)) * up
    zeros = jnp.zeros((out_ref.shape[0] - units, activation.shape[1]), jnp.float32)
    out_ref[...] = jnp.concatenate([activation, zeros], axis=0).astype(jnp.bfloat16)


def call(kernel, outs, name, *args, hbm=(), scratch=()):
    spec = lambda i: pl.BlockSpec(memory_space=pl.ANY if i in hbm else pltpu.VMEM)
    return pl.pallas_call(
        kernel,
        out_shape=outs,
        in_specs=[spec(i) for i in range(len(args))],
        scratch_shapes=scratch,
        compiler_params=pltpu.CompilerParams(vmem_limit_bytes=(56 if hbm else 32) * MIB),
        name=name,
    )(*args)


def exchange(x, groups):
    return lax.all_to_all(x, "seq", 0, 0, axis_index_groups=groups, tiled=True)


def gather(x, axis, count, groups=None):
    copies = jnp.broadcast_to(x, (count,) + x.shape)
    return lax.all_to_all(copies, axis, 0, 0, axis_index_groups=groups, tiled=True)


def on_device(n_kvh, queries, new_keys, new_values, prefix_keys, prefix_values, suffix_keys,
              suffix_values, prefix_offsets, suffix_lengths, out_weight, residual, norm_gain,
              w_gate, w_up, w_down):
    branches, width = residual.shape
    heads = queries.shape[1] // HD
    bands = SIDE
    band = branches // bands
    rows = heads * band
    tail_rows = band * suffix_keys.shape[1]
    hidden_units = w_gate.shape[1]
    units = hidden_units // SIDE**2
    pad = -(-units // 16) * 16
    bf16 = lambda *shape: jax.ShapeDtypeStruct(shape, jnp.bfloat16)
    like = lambda a: pltpu.VMEM(a.shape, a.dtype)
    copies_sem = lambda n: pltpu.SemaphoreType.DMA((n, PIECES))

    message = call(
        functools.partial(attend, bands, band, heads),
        bf16(SIDE * SIDE, band + STATS, HD),
        "attend",
        prefix_offsets.reshape(1, branches), suffix_lengths.reshape(1, branches), queries,
        prefix_keys, prefix_values, suffix_keys, suffix_values,
        hbm=(2, 3, 4, 5, 6),
        scratch=[like(queries), like(prefix_keys), like(prefix_values), like(suffix_keys),
                 like(suffix_values),
                 pltpu.VMEM((HD + EXTRA, prefix_keys.shape[0]), jnp.bfloat16),
                 pltpu.VMEM((bands, rows), jnp.int32), pltpu.VMEM((bands, rows), jnp.int32),
                 pltpu.VMEM((tail_rows, rows), jnp.int32),
                 pltpu.VMEM((bands // 2, prefix_keys.shape[0], 2 * rows), jnp.bfloat16),
                 pltpu.VMEM((bands, tail_rows, rows), jnp.bfloat16),
                 pltpu.VMEM((bands, rows), jnp.float32),
                 copies_sem(5)],
    )
    message, *moved = lax.optimization_barrier((message, w_gate, w_up))
    block = hidden_units // QUAD
    mine = call(arrange, (bf16(2, width, block),) * QUAD, "arrange", *moved)
    swap = lambda x, k: lax.ppermute(
        x, "seq", [(seq_at(p, q), seq_at(p ^ k, q)) for q in range(BLOCKS) for p in range(QUAD)]
    )
    both = [mine[0]] + [swap(mine[k], k) for k in range(1, QUAD)]

    own = call(
        functools.partial(finish, heads, band), bf16(SIDE * SIDE, band, HD), "finish",
        exchange(message, None), queries, new_keys, new_values,
        scratch=[pltpu.VMEM((rows, HD), jnp.float32)],
    )
    gathered = exchange(own, None)
    attention = (
        gathered.reshape(bands, heads, band, HD).transpose(0, 2, 1, 3).reshape(branches, heads * HD)
    )

    projected = jnp.dot(attention, out_weight, preferred_element_type=jnp.float32)
    hidden, message = call(
        combine, (bf16(branches, width), bf16(QUAD, branches + EXTRA, width)), "combine",
        gather(projected.astype(jnp.bfloat16), "kvh", n_kvh), residual, norm_gain.reshape(1, width),
    )
    message, *both = lax.optimization_barrier((message, *both))
    message = call(
        functools.partial(gate_up, units), bf16(BLOCKS, 2 * units + STATS, branches), "gate_up",
        exchange(message, P_GROUPS), *both,
    )
    activation = call(
        functools.partial(activate, units), bf16(pad, branches), "activate",
        exchange(message, Q_GROUPS),
    )[:units]
    activations = gather(activation, "seq", SIDE * SIDE, [SEQ_ORDER]).reshape(hidden_units, branches)
    ffn_part = lax.dot_general(
        activations, w_down, (((0,), (0,)), ((), ())), preferred_element_type=jnp.float32
    )
    terms = gather(ffn_part.astype(jnp.bfloat16), "kvh", n_kvh)
    ffn_sum = jnp.sum(terms.astype(jnp.float32), axis=0)
    mixed = (hidden.astype(jnp.float32) + ffn_sum).astype(jnp.bfloat16)
    return (attention, mixed)


def solution(mesh):
    return jax.shard_map(
        functools.partial(on_device, mesh.shape["kvh"]),
        mesh=mesh,
        in_specs=(
            P(None, "kvh"),
            P(None, "kvh"),
            P(None, "kvh"),
            P("seq", "kvh"),
            P("seq", "kvh"),
            P(None, "seq", "kvh"),
            P(None, "seq", "kvh"),
            P(),
            P(),
            P("kvh", "seq"),
            P(None, "seq"),
            P("seq"),
            P("seq", "kvh"),
            P("seq", "kvh"),
            P("kvh", "seq"),
        ),
        out_specs=(P(None, "kvh"), P(None, "seq")),
        check_vma=False,
    )
```

```python
import functools
import math

import jax
import jax.numpy as jnp
from jax import lax
from jax.experimental import pallas as pl
from jax.experimental.pallas import tpu as pltpu
from jax.sharding import PartitionSpec as P

HD = 128
D = 8192
SIDE = 8
QUAD = 4
BLOCKS = SIDE * SIDE // QUAD


def seq_at(p, q):
    return (q // (SIDE // 2) * 2 + p // 2) * SIDE + q % (SIDE // 2) * 2 + p % 2


P_GROUPS = [[seq_at(p, q) for p in range(QUAD)] for q in range(BLOCKS)]
Q_GROUPS = [[seq_at(p, q) for q in range(BLOCKS)] for p in range(QUAD)]
SEQ_ORDER = [seq_at(p, q) for p in range(QUAD) for q in range(BLOCKS)]
NEG_FILL = -1e30
EPSILON = 1e-05
SCALE_LOG2 = math.log2(math.e) / math.sqrt(HD)
STATS = 8
EXTRA = 16
PIECES = 4
MIB = 2**20


def dot_nt(a, b):
    return lax.dot_general(a, b, (((1,), (1,)), ((), ())), preferred_element_type=jnp.float32)


def parts_of(x, count):
    parts = []
    for _ in range(count):
        part = x.astype(jnp.bfloat16).astype(jnp.float32)
        parts.append(part)
        x = x - part
    return parts


def padded(rows, count):
    return jnp.concatenate(rows + [jnp.zeros_like(rows[0])] * (count - len(rows)), axis=0)


def with_ones(values):
    return jnp.concatenate([values.T, jnp.ones((EXTRA, values.shape[0]), values.dtype)], axis=0)


def bring(sources, targets, sems):
    waits = []
    for i, (source, target) in enumerate(zip(sources, targets)):
        size = source.shape[0] // PIECES
        copies = []
        for j in range(PIECES):
            part = pl.ds(j * size, size)
            copy = pltpu.make_async_copy(source.at[part], target.at[part], sems.at[i, j])
            copy.start()
            copies.append(copy)
        waits.append(lambda copies=copies: [copy.wait() for copy in copies])
    return waits


def own_place():
    seq = lax.axis_index("seq")
    return seq // SIDE % 2 * 2 + seq % 2


def head_rows(block, heads):
    return jnp.concatenate([block[:, h * HD : (h + 1) * HD] for h in range(heads)], axis=0)


def over(x, power):
    assert power & (power - 1) == 0
    return lax.shift_right_logical(x, power.bit_length() - 1)


def by_column(bands, band, numbers, shifts):
    size = numbers.shape[1]
    lane = lax.broadcasted_iota(jnp.int32, (bands, size), 1)
    mine = over(lane, band) == lax.broadcasted_iota(jnp.int32, (bands, size), 0)
    digits = []
    for i, shift in enumerate(shifts):
        digit = lax.shift_right_logical(numbers, shift)
        if i > 0:
            digit = digit & 31
        digits.append(jnp.where(mine, digit.astype(jnp.float32), 0.0))
    row = lax.broadcasted_iota(jnp.int32, (size, size), 0)
    col = lax.broadcasted_iota(jnp.int32, (size, size), 1)
    spread = jnp.where(row & (band - 1) == col & (band - 1), 1.0, 0.0).astype(jnp.bfloat16)
    got = jnp.dot(
        jnp.concatenate(digits, axis=0).astype(jnp.bfloat16), spread,
        preferred_element_type=jnp.float32,
    ).astype(jnp.int32)
    return sum(got[i * bands : (i + 1) * bands] << shift for i, shift in enumerate(shifts))


def attend(bands, band, heads, offsets_ref, lengths_ref, q_hbm, k_hbm, v_hbm, sk_hbm, sv_hbm, out_ref,
           q_ref, k_ref, v_ref, sk_ref, sv_ref, vt_ref, off_ref, len_ref, tail_pos_ref,
           weight_ref, tail_weight_ref, peak_ref, sems):
    context = k_ref.shape[0]
    tail = sk_ref.shape[1]
    cols = heads * band
    seq = lax.axis_index("seq")
    waits = bring(
        (q_hbm, k_hbm, sk_hbm, v_hbm, sv_hbm), (q_ref, k_ref, sk_ref, v_ref, sv_ref), sems
    )
    off_ref[...] = by_column(bands, band, offsets_ref[...], (10, 5, 0))
    len_ref[...] = by_column(bands, band, lengths_ref[...], (5, 0))
    row = lax.broadcasted_iota(jnp.int32, tail_pos_ref.shape, 0)
    col = lax.broadcasted_iota(jnp.int32, tail_pos_ref.shape, 1)
    own_branch = over(row, tail) == col & (band - 1)
    tail_pos_ref[...] = jnp.where(own_branch, row & (tail - 1), 2**20)

    def queries_of(g):
        return head_rows(q_ref[pl.ds(pl.multiple_of(g * band, band), band), :], heads)

    def weigh(p, first):
        bases = (2 * p, 2 * p + 1)
        if first:
            waits[0]()
        qs = [queries_of(g) for g in bases]
        both = jnp.concatenate(qs, axis=0)
        offset = jnp.concatenate([off_ref[pl.ds(g, 1), :] for g in bases], axis=1)
        if first:
            waits[1]()
        scores = dot_nt(k_ref[...], both)
        pos = lax.broadcasted_iota(jnp.int32, scores.shape, 0)
        scores = jnp.where(pos < offset - seq * context, scores, NEG_FILL)
        peak = jnp.max(scores, axis=0, keepdims=True)
        tails = []
        if first:
            waits[2]()
        for i, g in enumerate(bases):
            at = pl.multiple_of(g * band, band)
            keys = sk_ref[pl.ds(at, band)].reshape(band * tail, HD)
            tail_scores = dot_nt(keys, qs[i])
            length = len_ref[pl.ds(g, 1), :] - seq * tail
            tails.append(jnp.where(tail_pos_ref[...] < length, tail_scores, NEG_FILL))
        tail_peak = jnp.concatenate([jnp.max(t, axis=0, keepdims=True) for t in tails], axis=1)
        peak = jnp.maximum(peak, tail_peak)
        weight_ref[p] = jnp.exp2((scores - peak) * SCALE_LOG2).astype(jnp.bfloat16)
        for i, g in enumerate(bases):
            own_peak = peak[:, i * cols : (i + 1) * cols]
            peak_ref[pl.ds(g, 1), :] = own_peak
            tail_weight_ref[g] = jnp.exp2((tails[i] - own_peak) * SCALE_LOG2).astype(jnp.bfloat16)

    def add_up(p):
        sums = jnp.dot(vt_ref[...], weight_ref[p], preferred_element_type=jnp.float32)
        for i, g in enumerate((2 * p, 2 * p + 1)):
            at = pl.multiple_of(g * band, band)
            values = with_ones(sv_ref[pl.ds(at, band)].reshape(band * tail, HD))
            full = sums[:, i * cols : (i + 1) * cols] + jnp.dot(
                values, tail_weight_ref[g], preferred_element_type=jnp.float32
            )
            own_peak = peak_ref[pl.ds(g, 1), :]
            some = own_peak > 0.5 * NEG_FILL
            total = jnp.where(some, full[HD : HD + 1], 0.0)
            output = jnp.where(some, full[:HD], 0.0).T
            stats = padded(parts_of(own_peak, 3) + parts_of(total, 2), STATS)
            for h in range(heads):
                message = jnp.concatenate([output[h * band : (h + 1) * band], stats], axis=0)
                out_ref[g * heads + h] = message.astype(jnp.bfloat16)

    weigh(0, True)
    pl.loop(1, bands // 2)(lambda p: weigh(p, False))
    waits[3]()
    vt_ref[...] = with_ones(v_ref[...])
    waits[4]()
    pl.loop(0, bands // 2)(add_up)


def finish(heads, band, got_ref, q_ref, nk_ref, nv_ref, out_ref, columns_ref):
    count = got_ref.shape[0]
    seq = lax.axis_index("seq")
    own_band, own_head = seq // heads, seq % heads
    got = got_ref[...].astype(jnp.float32)
    stats = got[:, band:]
    kind = lax.broadcasted_iota(jnp.int32, stats.shape, 1)
    peaks = jnp.sum(jnp.where(kind < 3, stats, 0.0), axis=1)
    totals = jnp.sum(jnp.where(kind >= 3, stats, 0.0), axis=1)
    peak = jnp.max(peaks, axis=0, keepdims=True)
    factors = jnp.exp2((peaks - peak) * SCALE_LOG2)
    total = jnp.sum(factors * totals, axis=0, keepdims=True)
    zeros = jnp.zeros((peaks.shape[1] - count - 2, peaks.shape[1]), jnp.float32)
    columns_ref[...] = jnp.concatenate([factors, peak, total, zeros], axis=0).T
    columns = columns_ref[pl.ds(pl.multiple_of(own_head * band, band), band), :]
    output = sum(columns[:, s : s + 1] * got[s, :band] for s in range(count))
    peak, total = columns[:, count : count + 1], columns[:, count + 1 : count + 2]
    own = pl.ds(pl.multiple_of(own_band * band, band), band)
    query = q_ref[own, pl.ds(pl.multiple_of(own_head * HD, HD), HD)].astype(jnp.float32)
    fresh = jnp.sum(query * nk_ref[own, :].astype(jnp.float32), axis=1, keepdims=True)
    row_peak = jnp.maximum(peak, fresh)
    factor = jnp.exp2((peak - row_peak) * SCALE_LOG2)
    fresh_factor = jnp.exp2((fresh - row_peak) * SCALE_LOG2)
    numerator = factor * output + fresh_factor * nv_ref[own, :].astype(jnp.float32)
    attention = (numerator / (factor * total + fresh_factor)).astype(jnp.bfloat16)
    for i in range(out_ref.shape[0]):
        out_ref[i] = attention


def arrange(gate_ref, up_ref, *outs):
    block = outs[0].shape[2]
    for k in range(QUAD):
        columns = pl.ds(pl.multiple_of((own_place() ^ k) * block, HD), block)
        outs[k][0] = gate_ref[:, columns]
        outs[k][1] = up_ref[:, columns]


def combine(got_ref, residual_ref, gain_ref, hidden_ref, out_ref):
    projected = sum(got_ref[k].astype(jnp.float32) for k in range(got_ref.shape[0]))
    hidden = (residual_ref[...].astype(jnp.float32) + projected).astype(jnp.bfloat16)
    hidden_ref[...] = hidden
    wide = hidden.astype(jnp.float32)
    squares = jnp.sum((wide * wide).T, axis=0, keepdims=True)
    message = jnp.concatenate(
        [wide * gain_ref[...], padded(parts_of(squares, 2), EXTRA)], axis=0
    ).astype(jnp.bfloat16)
    for p in range(QUAD):
        out_ref[p] = message


def gate_up(units, hidden_ref, *refs):
    weights, out_ref = refs[:QUAD], refs[QUAD]
    place = own_place()
    rows = hidden_ref.shape[1] - EXTRA
    totals = [None, None]
    squares = None
    for k in range(QUAD):
        message = hidden_ref[place ^ k]
        hidden = message[:rows]
        extra = message[rows:].astype(jnp.float32)
        row = extra[0:1] + extra[1:2]
        squares = row if squares is None else squares + row
        for i in range(2):
            term = jnp.dot(hidden, weights[k][i], preferred_element_type=jnp.float32)
            totals[i] = term if totals[i] is None else totals[i] + term
    gate, up = [total.T for total in totals]
    extra = padded(parts_of(squares, 2), EXTRA)
    for q in range(BLOCKS):
        part = slice(units * q, units * (q + 1))
        out_ref[q] = jnp.concatenate([gate[part], up[part], extra], axis=0).astype(jnp.bfloat16)


def activate(units, got_ref, out_ref):
    sums = sum(got_ref[q].astype(jnp.float32) for q in range(BLOCKS))
    mean_square = (sums[2 * units : 2 * units + 1] + sums[2 * units + 1 : 2 * units + 2]) / D
    inverse = lax.rsqrt(mean_square + EPSILON)
    gate, up = sums[:units] * inverse, sums[units : 2 * units] * inverse
    activation = gate / (1.0 + jnp.exp(-gate)) * up
    zeros = jnp.zeros((out_ref.shape[0] - units, activation.shape[1]), jnp.float32)
    out_ref[...] = jnp.concatenate([activation, zeros], axis=0).astype(jnp.bfloat16)


def call(kernel, outs, name, *args, hbm=(), scratch=()):
    spec = lambda i: pl.BlockSpec(memory_space=pl.ANY if i in hbm else pltpu.VMEM)
    return pl.pallas_call(
        kernel,
        out_shape=outs,
        in_specs=[spec(i) for i in range(len(args))],
        scratch_shapes=scratch,
        compiler_params=pltpu.CompilerParams(vmem_limit_bytes=(56 if hbm else 32) * MIB),
        name=name,
    )(*args)


def exchange(x, groups):
    return lax.all_to_all(x, "seq", 0, 0, axis_index_groups=groups, tiled=True)


def gather(x, axis, count, groups=None):
    copies = jnp.broadcast_to(x, (count,) + x.shape)
    return lax.all_to_all(copies, axis, 0, 0, axis_index_groups=groups, tiled=True)


def on_device(n_kvh, queries, new_keys, new_values, prefix_keys, prefix_values, suffix_keys,
              suffix_values, prefix_offsets, suffix_lengths, out_weight, residual, norm_gain,
              w_gate, w_up, w_down):
    branches, width = residual.shape
    heads = queries.shape[1] // HD
    bands = SIDE
    band = branches // bands
    rows = heads * band
    tail_rows = band * suffix_keys.shape[1]
    hidden_units = w_gate.shape[1]
    units = hidden_units // SIDE**2
    pad = -(-units // 16) * 16
    bf16 = lambda *shape: jax.ShapeDtypeStruct(shape, jnp.bfloat16)
    like = lambda a: pltpu.VMEM(a.shape, a.dtype)
    copies_sem = lambda n: pltpu.SemaphoreType.DMA((n, PIECES))

    message = call(
        functools.partial(attend, bands, band, heads),
        bf16(SIDE * SIDE, band + STATS, HD),
        "attend",
        prefix_offsets.reshape(1, branches), suffix_lengths.reshape(1, branches), queries,
        prefix_keys, prefix_values, suffix_keys, suffix_values,
        hbm=(2, 3, 4, 5, 6),
        scratch=[like(queries), like(prefix_keys), like(prefix_values), like(suffix_keys),
                 like(suffix_values),
                 pltpu.VMEM((HD + EXTRA, prefix_keys.shape[0]), jnp.bfloat16),
                 pltpu.VMEM((bands, rows), jnp.int32), pltpu.VMEM((bands, rows), jnp.int32),
                 pltpu.VMEM((tail_rows, rows), jnp.int32),
                 pltpu.VMEM((bands // 2, prefix_keys.shape[0], 2 * rows), jnp.bfloat16),
                 pltpu.VMEM((bands, tail_rows, rows), jnp.bfloat16),
                 pltpu.VMEM((bands, rows), jnp.float32),
                 copies_sem(5)],
    )
    message, *moved = lax.optimization_barrier((message, w_gate, w_up))
    block = hidden_units // QUAD
    mine = call(arrange, (bf16(2, width, block),) * QUAD, "arrange", *moved)
    swap = lambda x, k: lax.ppermute(
        x, "seq", [(seq_at(p, q), seq_at(p ^ k, q)) for q in range(BLOCKS) for p in range(QUAD)]
    )
    both = [mine[0]] + [swap(mine[k], k) for k in range(1, QUAD)]

    own = call(
        functools.partial(finish, heads, band), bf16(SIDE * SIDE, band, HD), "finish",
        exchange(message, None), queries, new_keys, new_values,
        scratch=[pltpu.VMEM((rows, HD), jnp.float32)],
    )
    gathered = exchange(own, None)
    gathered, *both = lax.optimization_barrier((gathered, *both))
    by_branch = lambda a: (
        a.reshape(bands, heads, band, HD).transpose(0, 2, 1, 3).reshape(branches, heads * HD)
    )

    projected = jnp.dot(by_branch(gathered), out_weight, preferred_element_type=jnp.float32)
    hidden, message = call(
        combine, (bf16(branches, width), bf16(QUAD, branches + EXTRA, width)), "combine",
        gather(projected.astype(jnp.bfloat16), "kvh", n_kvh), residual, norm_gain.reshape(1, width),
    )
    hiddens, gathered = lax.optimization_barrier((exchange(message, P_GROUPS), gathered))
    attention = by_branch(gathered)
    message = call(
        functools.partial(gate_up, units), bf16(BLOCKS, 2 * units + EXTRA, branches), "gate_up",
        hiddens, *both,
    )
    activation = call(
        functools.partial(activate, units), bf16(pad, branches), "activate",
        exchange(message, Q_GROUPS),
    )[:units]
    activations = gather(activation, "seq", SIDE * SIDE, [SEQ_ORDER]).reshape(hidden_units, branches)
    ffn_part = lax.dot_general(
        activations, w_down, (((0,), (0,)), ((), ())), preferred_element_type=jnp.float32
    )
    terms = gather(ffn_part.astype(jnp.bfloat16), "kvh", n_kvh)
    ffn_sum = jnp.sum(terms.astype(jnp.float32), axis=0)
    mixed = (hidden.astype(jnp.float32) + ffn_sum).astype(jnp.bfloat16)
    return (attention, mixed)


def solution(mesh):
    return jax.shard_map(
        functools.partial(on_device, mesh.shape["kvh"]),
        mesh=mesh,
        in_specs=(
            P(None, "kvh"),
            P(None, "kvh"),
            P(None, "kvh"),
            P("seq", "kvh"),
            P("seq", "kvh"),
            P(None, "seq", "kvh"),
            P(None, "seq", "kvh"),
            P(),
            P(),
            P("kvh", "seq"),
            P(None, "seq"),
            P("seq"),
            P("seq", "kvh"),
            P("seq", "kvh"),
            P("kvh", "seq"),
        ),
        out_specs=(P(None, "kvh"), P(None, "seq")),
        check_vma=False,
    )
```

```python
import functools
import math

import jax
import jax.numpy as jnp
from jax import lax
from jax.experimental import pallas as pl
from jax.experimental.pallas import tpu as pltpu
from jax.sharding import PartitionSpec as P

HD = 128
D = 8192
SIDE = 8
Z_GROUPS = [[z * SIDE + y for z in range(SIDE)] for y in range(SIDE)]
Y_GROUPS = [[z * SIDE + y for y in range(SIDE)] for z in range(SIDE)]
QUAD = 4
BLOCKS = SIDE * SIDE // QUAD


def seq_at(p, q):
    return (q // (SIDE // 2) * 2 + p // 2) * SIDE + q % (SIDE // 2) * 2 + p % 2


P_GROUPS = [[seq_at(p, q) for p in range(QUAD)] for q in range(BLOCKS)]
Q_GROUPS = [[seq_at(p, q) for q in range(BLOCKS)] for p in range(QUAD)]
SEQ_ORDER = [seq_at(p, q) for p in range(QUAD) for q in range(BLOCKS)]
NEG_FILL = -1e30
EPSILON = 1e-05
SCALE_LOG2 = math.log2(math.e) / math.sqrt(HD)
EXTRA = 16
PIECES = 4
MIB = 2**20


def dot_nt(a, b):
    return lax.dot_general(a, b, (((1,), (1,)), ((), ())), preferred_element_type=jnp.float32)


def parts_of(x, count):
    parts = []
    for _ in range(count):
        part = x.astype(jnp.bfloat16).astype(jnp.float32)
        parts.append(part)
        x = x - part
    return parts


def padded(rows, count):
    return jnp.concatenate(rows + [jnp.zeros_like(rows[0])] * (count - len(rows)), axis=0)


def with_ones(values):
    return jnp.concatenate([values.T, jnp.ones((EXTRA, values.shape[0]), values.dtype)], axis=0)


def bring(sources, targets, sems):
    waits = []
    for i, (source, target) in enumerate(zip(sources, targets)):
        size = source.shape[0] // PIECES
        copies = []
        for j in range(PIECES):
            part = pl.ds(j * size, size)
            copy = pltpu.make_async_copy(source.at[part], target.at[part], sems.at[i, j])
            copy.start()
            copies.append(copy)
        waits.append(lambda copies=copies: [copy.wait() for copy in copies])
    return waits


def own_place():
    seq = lax.axis_index("seq")
    return seq // SIDE % 2 * 2 + seq % 2


def head_rows(block, heads):
    return jnp.concatenate([block[:, h * HD : (h + 1) * HD] for h in range(heads)], axis=0)


def over(x, power):
    assert power & (power - 1) == 0
    return lax.shift_right_logical(x, power.bit_length() - 1)


def by_column(bands, band, numbers, shifts):
    size = numbers.shape[1]
    lane = lax.broadcasted_iota(jnp.int32, (bands, size), 1)
    mine = over(lane, band) == lax.broadcasted_iota(jnp.int32, (bands, size), 0)
    digits = []
    for i, shift in enumerate(shifts):
        digit = lax.shift_right_logical(numbers, shift)
        if i > 0:
            digit = digit & 31
        digits.append(jnp.where(mine, digit.astype(jnp.float32), 0.0))
    row = lax.broadcasted_iota(jnp.int32, (size, size), 0)
    col = lax.broadcasted_iota(jnp.int32, (size, size), 1)
    spread = jnp.where(row & (band - 1) == col & (band - 1), 1.0, 0.0).astype(jnp.bfloat16)
    got = jnp.dot(
        jnp.concatenate(digits, axis=0).astype(jnp.bfloat16), spread,
        preferred_element_type=jnp.float32,
    ).astype(jnp.int32)
    return sum(got[i * bands : (i + 1) * bands] << shift for i, shift in enumerate(shifts))


def attend(bands, band, heads, offsets_ref, lengths_ref, q_hbm, k_hbm, v_hbm, sk_hbm, sv_hbm, out_ref,
           q_ref, k_ref, v_ref, sk_ref, sv_ref, vt_ref, off_ref, len_ref, tail_pos_ref,
           weight_ref, tail_weight_ref, peak_ref, sems):
    context = k_ref.shape[0]
    tail = sk_ref.shape[1]
    cols = heads * band
    seq = lax.axis_index("seq")
    waits = bring(
        (q_hbm, k_hbm, sk_hbm, v_hbm, sv_hbm), (q_ref, k_ref, sk_ref, v_ref, sv_ref), sems
    )
    off_ref[...] = by_column(bands, band, offsets_ref[...], (10, 5, 0))
    len_ref[...] = by_column(bands, band, lengths_ref[...], (5, 0))
    row = lax.broadcasted_iota(jnp.int32, tail_pos_ref.shape, 0)
    col = lax.broadcasted_iota(jnp.int32, tail_pos_ref.shape, 1)
    own_branch = over(row, tail) == col & (band - 1)
    tail_pos_ref[...] = jnp.where(own_branch, row & (tail - 1), 2**20)

    def queries_of(g):
        return head_rows(q_ref[pl.ds(pl.multiple_of(g * band, band), band), :], heads)

    def weigh(p, first):
        bases = (2 * p, 2 * p + 1)
        if first:
            waits[0]()
        qs = [queries_of(g) for g in bases]
        both = jnp.concatenate(qs, axis=0)
        offset = jnp.concatenate([off_ref[pl.ds(g, 1), :] for g in bases], axis=1)
        if first:
            waits[1]()
        scores = dot_nt(k_ref[...], both)
        pos = lax.broadcasted_iota(jnp.int32, scores.shape, 0)
        scores = jnp.where(pos < offset - seq * context, scores, NEG_FILL)
        peak = jnp.max(scores, axis=0, keepdims=True)
        tails = []
        if first:
            waits[2]()
        for i, g in enumerate(bases):
            at = pl.multiple_of(g * band, band)
            keys = sk_ref[pl.ds(at, band)].reshape(band * tail, HD)
            tail_scores = dot_nt(keys, qs[i])
            length = len_ref[pl.ds(g, 1), :] - seq * tail
            tails.append(jnp.where(tail_pos_ref[...] < length, tail_scores, NEG_FILL))
        tail_peak = jnp.concatenate([jnp.max(t, axis=0, keepdims=True) for t in tails], axis=1)
        peak = jnp.maximum(peak, tail_peak)
        weight_ref[p] = jnp.exp2((scores - peak) * SCALE_LOG2).astype(jnp.bfloat16)
        for i, g in enumerate(bases):
            own_peak = peak[:, i * cols : (i + 1) * cols]
            peak_ref[pl.ds(g, 1), :] = own_peak
            tail_weight_ref[g] = jnp.exp2((tails[i] - own_peak) * SCALE_LOG2).astype(jnp.bfloat16)

    def add_up(p):
        sums = jnp.dot(vt_ref[...], weight_ref[p], preferred_element_type=jnp.float32)
        for i, g in enumerate((2 * p, 2 * p + 1)):
            at = pl.multiple_of(g * band, band)
            values = with_ones(sv_ref[pl.ds(at, band)].reshape(band * tail, HD))
            full = sums[:, i * cols : (i + 1) * cols] + jnp.dot(
                values, tail_weight_ref[g], preferred_element_type=jnp.float32
            )
            own_peak = peak_ref[pl.ds(g, 1), :]
            some = own_peak > 0.5 * NEG_FILL
            total = jnp.where(some, full[HD : HD + 1], 0.0)
            output = jnp.where(some, full[:HD], 0.0).T
            stats = padded(parts_of(own_peak, 3) + parts_of(total, 2), EXTRA)
            out_ref[g] = jnp.concatenate([output, stats], axis=0).astype(jnp.bfloat16)

    weigh(0, True)
    pl.loop(1, bands // 2)(lambda p: weigh(p, False))
    waits[3]()
    vt_ref[...] = with_ones(v_ref[...])
    waits[4]()
    pl.loop(0, bands // 2)(add_up)


def merged(got_ref):
    count, rows = got_ref.shape[0], got_ref.shape[1] - EXTRA
    stats = [got_ref[s, rows:].astype(jnp.float32) for s in range(count)]
    peaks = [st[0:1] + st[1:2] + st[2:3] for st in stats]
    totals = [st[3:4] + st[4:5] for st in stats]
    peak = functools.reduce(jnp.maximum, peaks)
    factors = [jnp.exp2((p - peak) * SCALE_LOG2) for p in peaks]
    total = sum(f * t for f, t in zip(factors, totals))
    columns = padded(factors + [peak, total], rows).T
    output = sum(
        columns[:, s : s + 1] * got_ref[s, :rows].astype(jnp.float32) for s in range(count)
    )
    return output, peak, total, columns[:, count : count + 1], columns[:, count + 1 : count + 2]


def merge(got_ref, out_ref):
    output, peak, total, _, _ = merged(got_ref)
    stats = padded(parts_of(peak, 3) + parts_of(total, 2), EXTRA)
    message = jnp.concatenate([output, stats], axis=0).astype(jnp.bfloat16)
    for i in range(out_ref.shape[0]):
        out_ref[i] = message


def finish(heads, band, got_ref, q_ref, nk_ref, nv_ref, out_ref):
    output, _, _, peak, total = merged(got_ref)
    own = pl.ds(pl.multiple_of(lax.axis_index("seq") // SIDE * band, band), band)
    tiled = lambda ref: jnp.concatenate([ref[own, :].astype(jnp.float32)] * heads, axis=0)
    query = head_rows(q_ref[own, :], heads).astype(jnp.float32)
    fresh = jnp.sum(query * tiled(nk_ref), axis=1, keepdims=True)
    row_peak = jnp.maximum(peak, fresh)
    factor = jnp.exp2((peak - row_peak) * SCALE_LOG2)
    fresh_factor = jnp.exp2((fresh - row_peak) * SCALE_LOG2)
    numerator = factor * output + fresh_factor * tiled(nv_ref)
    attention = (numerator / (factor * total + fresh_factor)).astype(jnp.bfloat16)
    for i in range(out_ref.shape[0]):
        out_ref[i] = attention


def arrange(gate_ref, up_ref, *outs):
    block = outs[0].shape[2]
    for k in range(QUAD):
        columns = pl.ds(pl.multiple_of((own_place() ^ k) * block, HD), block)
        outs[k][0] = gate_ref[:, columns]
        outs[k][1] = up_ref[:, columns]


def combine(got_ref, residual_ref, gain_ref, hidden_ref, out_ref):
    projected = sum(got_ref[k].astype(jnp.float32) for k in range(got_ref.shape[0]))
    hidden = (residual_ref[...].astype(jnp.float32) + projected).astype(jnp.bfloat16)
    hidden_ref[...] = hidden
    wide = hidden.astype(jnp.float32)
    squares = jnp.sum((wide * wide).T, axis=0, keepdims=True)
    message = jnp.concatenate(
        [wide * gain_ref[...], padded(parts_of(squares, 2), EXTRA)], axis=0
    ).astype(jnp.bfloat16)
    for p in range(QUAD):
        out_ref[p] = message


def gate_up(units, hidden_ref, *refs):
    weights, out_ref = refs[:QUAD], refs[QUAD]
    place = own_place()
    rows = hidden_ref.shape[1] - EXTRA
    totals = [None, None]
    squares = None
    for k in range(QUAD):
        message = hidden_ref[place ^ k]
        hidden = message[:rows]
        extra = message[rows:].astype(jnp.float32)
        row = extra[0:1] + extra[1:2]
        squares = row if squares is None else squares + row
        for i in range(2):
            term = jnp.dot(hidden, weights[k][i], preferred_element_type=jnp.float32)
            totals[i] = term if totals[i] is None else totals[i] + term
    gate, up = [total.T for total in totals]
    extra = padded(parts_of(squares, 2), EXTRA)
    for q in range(BLOCKS):
        part = slice(units * q, units * (q + 1))
        out_ref[q] = jnp.concatenate([gate[part], up[part], extra], axis=0).astype(jnp.bfloat16)


def activate(units, got_ref, out_ref):
    sums = sum(got_ref[q].astype(jnp.float32) for q in range(BLOCKS))
    mean_square = (sums[2 * units : 2 * units + 1] + sums[2 * units + 1 : 2 * units + 2]) / D
    inverse = lax.rsqrt(mean_square + EPSILON)
    gate, up = sums[:units] * inverse, sums[units : 2 * units] * inverse
    activation = gate / (1.0 + jnp.exp(-gate)) * up
    zeros = jnp.zeros((out_ref.shape[0] - units, activation.shape[1]), jnp.float32)
    out_ref[...] = jnp.concatenate([activation, zeros], axis=0).astype(jnp.bfloat16)


def call(kernel, outs, name, *args, hbm=(), scratch=()):
    spec = lambda i: pl.BlockSpec(memory_space=pl.ANY if i in hbm else pltpu.VMEM)
    return pl.pallas_call(
        kernel,
        out_shape=outs,
        in_specs=[spec(i) for i in range(len(args))],
        scratch_shapes=scratch,
        compiler_params=pltpu.CompilerParams(vmem_limit_bytes=(56 if hbm else 32) * MIB),
        name=name,
    )(*args)


def exchange(x, groups):
    return lax.all_to_all(x, "seq", 0, 0, axis_index_groups=groups, tiled=True)


def gather(x, axis, count, groups=None):
    copies = jnp.broadcast_to(x, (count,) + x.shape)
    return lax.all_to_all(copies, axis, 0, 0, axis_index_groups=groups, tiled=True)


def on_device(n_kvh, queries, new_keys, new_values, prefix_keys, prefix_values, suffix_keys,
              suffix_values, prefix_offsets, suffix_lengths, out_weight, residual, norm_gain,
              w_gate, w_up, w_down):
    branches, width = residual.shape
    heads = queries.shape[1] // HD
    bands = SIDE
    band = branches // bands
    rows = heads * band
    tail_rows = band * suffix_keys.shape[1]
    hidden_units = w_gate.shape[1]
    units = hidden_units // SIDE**2
    pad = -(-units // 16) * 16
    bf16 = lambda *shape: jax.ShapeDtypeStruct(shape, jnp.bfloat16)
    like = lambda a: pltpu.VMEM(a.shape, a.dtype)
    copies_sem = lambda n: pltpu.SemaphoreType.DMA((n, PIECES))

    message = call(
        functools.partial(attend, bands, band, heads),
        bf16(bands, rows + EXTRA, HD),
        "attend",
        prefix_offsets.reshape(1, branches), suffix_lengths.reshape(1, branches), queries,
        prefix_keys, prefix_values, suffix_keys, suffix_values,
        hbm=(2, 3, 4, 5, 6),
        scratch=[like(queries), like(prefix_keys), like(prefix_values), like(suffix_keys),
                 like(suffix_values),
                 pltpu.VMEM((HD + EXTRA, prefix_keys.shape[0]), jnp.bfloat16),
                 pltpu.VMEM((bands, rows), jnp.int32), pltpu.VMEM((bands, rows), jnp.int32),
                 pltpu.VMEM((tail_rows, rows), jnp.int32),
                 pltpu.VMEM((bands // 2, prefix_keys.shape[0], 2 * rows), jnp.bfloat16),
                 pltpu.VMEM((bands, tail_rows, rows), jnp.bfloat16),
                 pltpu.VMEM((bands, rows), jnp.float32),
                 copies_sem(5)],
    )
    message, *moved = lax.optimization_barrier((message, w_gate, w_up))
    block = hidden_units // QUAD
    mine = call(arrange, (bf16(2, width, block),) * QUAD, "arrange", *moved)
    swap = lambda x, k: lax.ppermute(
        x, "seq", [(seq_at(p, q), seq_at(p ^ k, q)) for q in range(BLOCKS) for p in range(QUAD)]
    )
    both = [mine[0]] + [swap(mine[k], k) for k in range(1, QUAD)]

    message = call(merge, bf16(SIDE, rows + EXTRA, HD), "merge", exchange(message, Z_GROUPS))
    own = call(
        functools.partial(finish, heads, band), bf16(SIDE, rows, HD), "finish",
        exchange(message, Y_GROUPS), queries, new_keys, new_values,
    )
    gathered = exchange(own, Z_GROUPS)
    attention = (
        gathered.reshape(bands, heads, band, HD).transpose(0, 2, 1, 3).reshape(branches, heads * HD)
    )

    projected = jnp.dot(attention, out_weight, preferred_element_type=jnp.float32)
    hidden, message = call(
        combine, (bf16(branches, width), bf16(QUAD, branches + EXTRA, width)), "combine",
        gather(projected.astype(jnp.bfloat16), "kvh", n_kvh), residual, norm_gain.reshape(1, width),
    )
    message, *both = lax.optimization_barrier((message, *both))
    message = call(
        functools.partial(gate_up, units), bf16(BLOCKS, 2 * units + EXTRA, branches), "gate_up",
        exchange(message, P_GROUPS), *both,
    )
    activation = call(
        functools.partial(activate, units), bf16(pad, branches), "activate",
        exchange(message, Q_GROUPS),
    )[:units]
    activations = gather(activation, "seq", SIDE * SIDE, [SEQ_ORDER]).reshape(hidden_units, branches)
    ffn_part = lax.dot_general(
        activations, w_down, (((0,), (0,)), ((), ())), preferred_element_type=jnp.float32
    )
    terms = gather(ffn_part.astype(jnp.bfloat16), "kvh", n_kvh)
    ffn_sum = jnp.sum(terms.astype(jnp.float32), axis=0)
    mixed = (hidden.astype(jnp.float32) + ffn_sum).astype(jnp.bfloat16)
    return (attention, mixed)


def solution(mesh):
    return jax.shard_map(
        functools.partial(on_device, mesh.shape["kvh"]),
        mesh=mesh,
        in_specs=(
            P(None, "kvh"),
            P(None, "kvh"),
            P(None, "kvh"),
            P("seq", "kvh"),
            P("seq", "kvh"),
            P(None, "seq", "kvh"),
            P(None, "seq", "kvh"),
            P(),
            P(),
            P("kvh", "seq"),
            P(None, "seq"),
            P("seq"),
            P("seq", "kvh"),
            P("seq", "kvh"),
            P("kvh", "seq"),
        ),
        out_specs=(P(None, "kvh"), P(None, "seq")),
        check_vma=False,
    )
```
